32 devices in a mesh: groups: 2 (over x), head: 4 (over y, core), req: 4 (over z).
Axes of the slice: x: 2, y: 2, z: 4, core: 2. Of those that a mesh axis runs over, the one named last changes fastest.
Arguments:
- ssm_input: bfloat16 [16, 64, 4096], P(None, ('groups', 'req'), 'head'), parts along dimension 1, may hold values from -6 to 6
- write_vec: bfloat16 [16, 64, 128], P('head', ('groups', 'req')), parts along dimension 1, may hold values from -6 to 6
- read_vec: bfloat16 [16, 64, 128], P('head', ('groups', 'req')), parts along dimension 1, may hold values from -0.5 to 0.5
- step_raw: float32 [16, 64, 64], P(None, ('groups', 'req'), 'head'), parts along dimension 1, may hold values from -4 to 4
- step_bias: float32 [64], P('head'), may hold values from -3 to -0.5
- decay_rate: float32 [64], P('head'), may hold values from 1 to 16
- skip_gain: float32 [64], P('head'), may hold values from 0.5 to 1.5
- cache_state: bfloat16 [64, 64, 64, 128], P(('groups', 'req'), 'head'), parts along dimension 0, may hold values from -6 to 6
- parents: int32 [64, 16], P(('groups', 'req')), parts along dimension 0, may hold values from -1 to 14, as said below
- out_proj: bfloat16 [4096, 4096], P('head'), may hold values from -0.09375 to 0.09375
- residual: bfloat16 [16, 64, 4096], P('head', ('groups', 'req')), parts along dimension 1, may hold values from -6 to 6
- norm_gain: float32 [4096], replicated, may hold values from 0.1 to 1.9
- router: bfloat16 [4096, 64], replicated, may hold values from -0.09375 to 0.09375
- expert_ids: int32 [16, 64, 10], P('head', ('groups', 'req')), parts along dimension 1, may hold values from 0 to 63, as said below
- gate_proj: bfloat16 [128, 4096, 384], P(('head', 'req')), may hold values from -0.09375 to 0.09375
- up_proj: bfloat16 [128, 4096, 384], P(('head', 'req')), may hold values from -0.09375 to 0.09375
- down_proj: bfloat16 [128, 384, 4096], P(('head', 'req')), may hold values from -0.21875 to 0.21875
Outputs:
- layer_out: bfloat16 [16, 64, 4096], P('head', ('groups', 'req')), parts along dimension 1
The draws below stay inside these ranges and needn't reach their ends.
There are 2 independent parts, one for each index of `groups`. The reference program is written for one: setup_inputs(seed, part) draws one part's arguments, and reference() takes and returns one part's arrays. A program takes and returns all parts, laid end to end along the dimension named above; an argument that names none is the same for every part. Nothing has to cross between parts.
Inputs may be any that keep to these rules, and one draw needn't show every extreme that they name: parents[r, 0] = -1 (the root); for j >= 1, parents[r, j] lies in 0 to j - 1; the last node's parent is node 14. `expert_ids`: each row names 10 different experts. Within the rows of one device (an aligned block of the 4 node index or indices and 8 requests held there) every expert is named by 4 or by 8 rows, 16 experts by 8; one expert is named by 8 rows in every such block.
All inputs are finite; a program needn't handle non-finite values.
Results may differ from the reference program's by a relative error of at most 0.0058.
Values may be sent and summed in bfloat16 or wider, within the bound.
A program may use at most 192 MiB of HBM per device.

```python
import math
import jax
import jax.numpy as jnp
from jax import lax

D = 4096
NH = 64
P_SIZE = 64
N = 128
NODES = 16
TOPK = 10
EXPERTS = 64
FFE = 768
REQ_DEV = 8
REQS = 32
HALF = 384
NPD = 4
CAP = 8
N_HEAD = 4
N_REQ = 4


def draw_parents(key, part):
    labels = jnp.arange(NODES, dtype=jnp.int32)
    ceiling = jnp.maximum(labels, 1)
    drawn = jax.random.randint(jax.random.fold_in(key, 7), (REQS, NODES), 0, ceiling[None, :])
    chosen = jnp.where(labels[None, :] == 0, -1, drawn)
    chosen = jnp.where(labels[None, :] == NODES - 1, NODES - 2, chosen)
    return chosen.astype(jnp.int32)


def draw_expert_ids(key, part):
    spare = EXPERTS // 4
    cycle_length = EXPERTS + spare
    node_blocks = NODES // NPD
    req_blocks = REQS // REQ_DEV
    blocks = node_blocks * req_blocks
    per_block = NPD * REQ_DEV * TOPK
    labels = jnp.arange(EXPERTS, dtype=jnp.int32)
    scores = jax.random.randint(jax.random.fold_in(key, 21), (blocks, EXPERTS), 0, 1 << 20) * EXPERTS + labels[None, :]
    orders = jnp.argsort(scores, axis=1).astype(jnp.int32)
    favored = jax.random.randint(jax.random.fold_in(key, 22), (), 0, EXPERTS).astype(jnp.int32)
    leading = orders[:, :1]
    swapped = jnp.where(orders == favored, leading, orders)
    orders = jnp.where(labels[None, :] == 0, favored, swapped)
    cycle_list = jnp.concatenate([orders, orders[:, :spare]], axis=1)
    shifts = jax.random.randint(jax.random.fold_in(key, 23), (blocks, 1), 0, cycle_length)
    positions = jnp.arange(per_block, dtype=jnp.int32)
    picks = jnp.take_along_axis(cycle_list, (positions[None, :] + shifts) % cycle_length, axis=1)
    picks = picks.reshape(node_blocks, req_blocks, NPD, REQ_DEV, TOPK).transpose(0, 2, 1, 3, 4)
    return picks.reshape(NODES, REQS, TOPK).astype(jnp.int32)


def block_scale(own_key, extent, split, smallest, high):
    def one(axis_at, shards_of):
        steps = jax.random.uniform(jax.random.fold_in(jax.random.fold_in(own_key, 6), axis_at), (shards_of,), jnp.float32, smallest / len(split), high / len(split))
        return jnp.repeat(jnp.exp(steps), extent[axis_at] // shards_of).reshape((-1,) + (1,) * (len(extent) - axis_at - 1))

    gain = one(*split[0])
    for cut in split[1:]:
        gain = gain * one(*cut)
    return gain


def gaussian(rng, dims, scale, most, cuts=(), kind=jnp.bfloat16):
    values = jax.random.normal(rng, dims, jnp.float32) * scale
    if len(cuts) > 0:
        values = block_scale(rng, dims, cuts, -0.22, 0.18) * values
    return jnp.clip(values, min=-most, max=most).astype(kind)


def setup_inputs(seed: int = 0, part: int = 0) -> dict:
    keys = jax.random.split(jax.random.key(seed), 18)
    own_keys = jax.random.split(jax.random.fold_in(keys[17], part), 18)
    ssm_input = gaussian(own_keys[0], (NODES, REQS, NH * P_SIZE), 1.0, 6.0, ((1, 4), (2, 4)))
    write_vec = gaussian(own_keys[1], (NODES, REQS, N), 1.0, 6.0, ((0, 4), (1, 4)))
    read_vec = gaussian(own_keys[2], (NODES, REQS, N), N ** -0.5, 0.5, ((0, 4), (1, 4)))
    step_raw = gaussian(own_keys[3], (NODES, REQS, NH), 1.0, 4.0, ((1, 4), (2, 4)), jnp.float32)
    step_bias = jnp.clip(-3.0 + 2.5 * jax.random.uniform(keys[4], (NH,), jnp.float32) ** block_scale(keys[4], (NH,), ((0, 4),), -0.2, 0.2), -3.0, -0.5)
    decay_rate = jnp.clip(jnp.exp(math.log(16.0) - 2.7725887 * jax.random.uniform(keys[5], (NH,), jnp.float32) ** block_scale(keys[5], (NH,), ((0, 4),), -0.2, 0.2)), 1.0, 16.0)
    skip_gain = jnp.clip(0.5 + 1.0 * jax.random.uniform(keys[6], (NH,), jnp.float32) ** block_scale(keys[6], (NH,), ((0, 4),), -0.2, 0.2), 0.5, 1.5)
    cache_state = gaussian(own_keys[7], (REQS, NH, P_SIZE, N), 1.0, 6.0, ((0, 4), (1, 4)))
    parents = draw_parents(jax.random.fold_in(jax.random.fold_in(keys[17], part), 71), part)
    out_proj = gaussian(keys[9], (NH * P_SIZE, D), (NH * P_SIZE) ** -0.5, 0.09375, ((0, 4),))
    residual = gaussian(own_keys[10], (NODES, REQS, D), 1.0, 6.0, ((0, 4), (1, 4)))
    norm_gain = jnp.clip(1.0 + 0.18 * jax.random.normal(keys[11], (D,), jnp.float32), 0.1, 1.9)
    router = gaussian(keys[12], (D, EXPERTS), D ** -0.5, 0.09375)
    expert_ids = draw_expert_ids(jax.random.fold_in(jax.random.fold_in(keys[17], part), 71), part)
    gate_proj = gaussian(keys[14], (2 * EXPERTS, D, HALF), D ** -0.5, 0.09375, ((0, 16),))
    up_proj = gaussian(keys[15], (2 * EXPERTS, D, HALF), D ** -0.5, 0.09375, ((0, 16),))
    down_proj = gaussian(keys[16], (2 * EXPERTS, HALF, D), FFE ** -0.5, 0.21875, ((0, 16),))
    return dict(ssm_input=ssm_input, write_vec=write_vec, read_vec=read_vec, step_raw=step_raw, step_bias=step_bias, decay_rate=decay_rate, skip_gain=skip_gain, cache_state=cache_state, parents=parents, out_proj=out_proj, residual=residual, norm_gain=norm_gain, router=router, expert_ids=expert_ids, gate_proj=gate_proj, up_proj=up_proj, down_proj=down_proj)


def ancestry(parents):
    nodes = parents.shape[1]
    labels = jnp.arange(nodes, dtype=jnp.int32)
    parent_hot = (parents[:, :, None] == labels[None, None, :]).astype(jnp.float32)
    identity = jnp.broadcast_to(jnp.eye(nodes, dtype=jnp.float32), parent_hot.shape)

    def extend(turn, reach):
        return identity + jnp.einsum('rjk,rki->rji', parent_hot, reach, precision=lax.Precision.HIGHEST)
    return lax.fori_loop(0, nodes, extend, identity)

def reference(ssm_input, write_vec, read_vec, step_raw, step_bias, decay_rate, skip_gain, cache_state, parents, out_proj, residual, norm_gain, router, expert_ids, gate_proj, up_proj, down_proj):
    nodes, requests, columns = ssm_input.shape
    heads = step_raw.shape[2]
    head_size = columns // heads
    inputs4 = ssm_input.reshape(nodes, requests, heads, head_size)
    step = jax.nn.softplus(step_raw + step_bias)
    rates = -step * decay_rate
    reach = ancestry(parents)
    depth = jnp.einsum('rji,irh->jrh', reach, rates, precision=lax.Precision.HIGHEST)
    affinity = jnp.einsum('jrn,irn->rji', read_vec.astype(jnp.float32), write_vec.astype(jnp.float32), precision=lax.Precision.HIGHEST)
    by_request = depth.transpose(1, 0, 2)
    spread = by_request[:, :, None, :] - by_request[:, None, :, :]
    linked = reach[:, :, :, None] > 0
    factor = jnp.where(linked, jnp.exp(jnp.where(linked, spread, 0.0)), 0.0)
    weights = (factor * affinity[:, :, :, None] * step.transpose(1, 0, 2)[:, None, :, :]).astype(jnp.bfloat16)
    tree_part = jnp.einsum('rjih,irhp->jrhp', weights.astype(jnp.float32), inputs4.astype(jnp.float32), precision=lax.Precision.HIGHEST)
    cache_part = jnp.einsum('jrn,rhpn->jrhp', read_vec.astype(jnp.float32), cache_state.astype(jnp.float32), precision=lax.Precision.HIGHEST)
    cache_part = cache_part * jnp.exp(depth)[:, :, :, None]
    ssm_out = (tree_part + cache_part + skip_gain[:, None] * inputs4.astype(jnp.float32)).astype(jnp.bfloat16)
    ssm_out = ssm_out.reshape(nodes * requests, columns)
    mixed = jnp.dot(ssm_out, out_proj, preferred_element_type=jnp.float32)
    width = out_proj.shape[1]
    after_mixer = (residual.reshape(nodes * requests, width).astype(jnp.float32) + mixed).astype(jnp.bfloat16)
    widened = after_mixer.astype(jnp.float32)
    meansq = lax.optimization_barrier(jnp.mean(widened * widened, axis=-1, keepdims=True))
    normed = (widened * lax.rsqrt(meansq + 1e-05) * norm_gain).astype(jnp.bfloat16)
    choices_flat = expert_ids.reshape(nodes * requests, TOPK)
    logits = jnp.dot(normed, router, preferred_element_type=jnp.float32)
    picked_logits = jnp.take_along_axis(logits, choices_flat, axis=1)
    powered = jnp.exp(picked_logits)
    gate = (powered / lax.optimization_barrier(jnp.sum(powered, axis=1, keepdims=True))).astype(jnp.bfloat16)
    gate_wide = gate.astype(jnp.float32)
    limit = N_HEAD * N_REQ * CAP
    token_count = nodes * requests

    def visit(total, expert):
        chosen = choices_flat == expert
        present = jnp.any(chosen, axis=1)
        share = lax.optimization_barrier(jnp.sum(jnp.where(chosen, gate_wide, 0.0), axis=1))
        order = jnp.cumsum(present.astype(jnp.int32)) - 1
        target = jnp.where(present, order, limit).astype(jnp.int32)
        owner = jnp.zeros((limit,), jnp.int32).at[target].set(jnp.arange(token_count, dtype=jnp.int32), mode='drop')
        filled = jnp.zeros((limit,), jnp.float32).at[target].set(1.0, mode='drop')
        rows = jnp.where(filled[:, None] > 0, normed[owner], jnp.zeros((), jnp.bfloat16))
        halves = []
        for side in range(2):
            index = (side * EXPERTS + expert).astype(jnp.int32)
            gate_rows = lax.dynamic_index_in_dim(gate_proj, index, 0, keepdims=False)
            up_rows = lax.dynamic_index_in_dim(up_proj, index, 0, keepdims=False)
            down_rows = lax.dynamic_index_in_dim(down_proj, index, 0, keepdims=False)
            gated = jnp.dot(rows, gate_rows, preferred_element_type=jnp.float32)
            lifted = jnp.dot(rows, up_rows, preferred_element_type=jnp.float32)
            act = (jax.nn.silu(gated) * lifted).astype(jnp.bfloat16)
            halves.append(jnp.dot(act, down_rows, preferred_element_type=jnp.float32).astype(jnp.bfloat16))
        result = (halves[0].astype(jnp.float32) + halves[1].astype(jnp.float32)).astype(jnp.bfloat16)
        fetched = result[jnp.where(present, order, 0).astype(jnp.int32)].astype(jnp.float32)
        return (total + share[:, None] * fetched, None)
    moe, _ = lax.scan(visit, jnp.zeros((token_count, width), jnp.float32), jnp.arange(EXPERTS, dtype=jnp.int32))
    layer_out = (after_mixer.astype(jnp.float32) + moe).astype(jnp.bfloat16)
    return layer_out.reshape(nodes, requests, width)
```

```python
import functools
import jax
import jax.numpy as jnp
from jax import lax
from jax.experimental import pallas as pl
from jax.experimental.pallas import tpu as pltpu
from jax.sharding import PartitionSpec as P

F32 = jnp.float32
BF16 = jnp.bfloat16


def ancestry(parents):
    nodes = parents.shape[1]
    labels = jnp.arange(nodes, dtype=jnp.int32)
    power = (parents[:, :, None] == labels[None, None, :]).astype(BF16)
    reach = power + jnp.eye(nodes, dtype=BF16)
    covered = 2
    while covered < nodes:
        power = jnp.einsum("rjk,rki->rji", power, power, preferred_element_type=F32).astype(BF16)
        reach = reach + jnp.einsum("rjk,rki->rji", power, reach, preferred_element_type=F32).astype(BF16)
        covered *= 2
    return reach.astype(F32)


def remote(src, dst, send, recv, head, req):
    return pltpu.make_async_remote_copy(
        src_ref=src,
        dst_ref=dst,
        send_sem=send,
        recv_sem=recv,
        device_id={"head": head, "req": req},
        device_id_type=pl.DeviceIdType.MESH,
    )


def block_kernel(
    ys, zs, cap, chunks,
    part, res, gain, router, ids, wg_h, wu_h, wd_h,
    out,
    buf, wg, wu, wd, xs, act, cmat, gts, ybuf, pbuf, trecv, ysend, yrecv, zsend, zrecv, mt, ms, my, am,
    mt_s, mt_r, my_s, my_r, az_s, ay_s, at_s, ar, rt_s, rt_r, ry_s, ry_r, rz_s, rz_r, w_s, d_s,
):
    head = lax.axis_index("head")
    z = lax.axis_index("req")
    y = head // 2
    c = head % 2
    t = 1 - c
    twin = y * 2 + t
    rows, width = res.shape
    experts = router.shape[1]
    held, hidden = wg_h.shape[0], wg_h.shape[2]
    slots = wg.shape[0]
    dslots = wd.shape[0]
    tokens = 2 * ys * zs * rows
    cw = width // chunks

    def at_y(d):
        return (y + d) % ys

    flip = 1 - 2 * (2 * z // zs)

    def at_z(d):
        return (z + flip * d + zs) % zs

    def blk(yy, cc, zz):
        return (yy * 2 + cc) * zs + zz

    def load_gu(h, slot):
        return (
            pltpu.make_async_copy(wg_h.at[h], wg.at[slot], w_s.at[slot, 0]),
            pltpu.make_async_copy(wu_h.at[h], wu.at[slot], w_s.at[slot, 1]),
        )

    def load_d(k):
        return pltpu.make_async_copy(
            wd_h.at[:, :, pl.ds(k * cw, cw)], wd.at[k % dslots], d_s.at[k % dslots]
        )

    barrier = pltpu.get_barrier_semaphore()
    pl.semaphore_signal(barrier, inc=1, device_id={"head": twin, "req": z}, device_id_type=pl.DeviceIdType.MESH)
    for d in range(1, ys):
        pl.semaphore_signal(barrier, inc=1, device_id={"head": at_y(d) * 2 + c, "req": z}, device_id_type=pl.DeviceIdType.MESH)
    for d in range(1, zs):
        pl.semaphore_signal(barrier, inc=1, device_id={"head": head, "req": (z + d) % zs}, device_id_type=pl.DeviceIdType.MESH)
    pl.semaphore_wait(barrier, ys + zs - 1)

    pending = []
    twin_parts = []
    for d in [*range(1, ys), 0]:
        cp = remote(part.at[at_y(d), t], mt.at[d], mt_s.at[d], mt_r.at[d], twin, z)
        cp.start()
        twin_parts.append((d, cp))
    for h in range(slots):
        for cp in load_gu(h, h):
            cp.start()
    for k in range(dslots):
        load_d(k).start()
    for d, cp in twin_parts:
        cp.wait_recv()
        if d > 0:
            ms[d] = (part[at_y(d), c] + mt[d]).astype(BF16)
            yc = remote(ms.at[d], my.at[ys - d], my_s.at[d], my_r.at[ys - d], at_y(d) * 2 + c, z)
            yc.start()
            pending.append(yc)
        pending.append(cp)
    mixed = part[y, c] + mt[0]
    for r in range(1, ys):
        remote(ms.at[r], my.at[r], my_s.at[r], my_r.at[r], at_y(r) * 2 + c, z).wait_recv()
        mixed = mixed + my[r].astype(F32)
    after = (res[...].astype(F32) + mixed).astype(BF16)
    am[...] = after
    wide = after.astype(F32)
    meansq = jnp.mean(wide * wide, axis=-1, keepdims=True)
    normed = (wide * lax.rsqrt(meansq + 1e-05) * gain[...]).astype(BF16)
    own = blk(y, c, z)
    buf[own, :, :width] = normed
    logits = jnp.dot(normed, router[...], preferred_element_type=F32)
    lanes = lax.broadcasted_iota(jnp.int32, (rows, experts), 1)
    chosen = ids[...]
    named = lanes == chosen[:, 0:1]
    for k in range(1, ids.shape[1]):
        named = named | (lanes == chosen[:, k : k + 1])
    powered = jnp.where(named, jnp.exp(jnp.where(named, logits, 0.0)), 0.0)
    gate = powered / jnp.sum(powered, axis=1, keepdims=True)
    if experts < 128:
        gate = jnp.concatenate([gate, jnp.zeros((rows, 128 - experts), F32)], axis=1)
    buf[own, :, width:] = gate.astype(BF16)

    def pass_y(b, i):
        for d in range(1, ys):
            s = (d - 1) * zs + i
            cp = remote(buf.at[b], buf.at[b], ay_s.at[s], ar.at[b], at_y(d) * 2 + c, z)
            cp.start()
            pending.append(cp)

    def pass_twin(b, i):
        cp = remote(buf.at[b], buf.at[b], at_s.at[i], ar.at[b], twin, z)
        cp.start()
        pending.append(cp)

    def landed(b):
        remote(buf.at[b], buf.at[b], at_s.at[0], ar.at[b], twin, z).wait_recv()

    pass_y(own, 0)
    for d in range(1, zs):
        cp = remote(buf.at[own], buf.at[own], az_s.at[d], ar.at[own], head, at_z(d))
        cp.start()
        pending.append(cp)
    pass_twin(own, 0)
    for d in range(1, zs):
        b = blk(y, c, at_z(d))
        landed(b)
        pass_y(b, d)
        pass_twin(b, d)
    for e in range(1, ys):
        for d in range(zs):
            b = blk(at_y(e), c, at_z(d))
            landed(b)
            pass_twin(b, e * zs + d)
    for e in range(ys):
        for d in range(zs):
            landed(blk(at_y(e), t, at_z(d)))

    gates = buf[:, :, width:].reshape(tokens, 128)
    first = ((head * zs + z) * held) % experts
    row_of = lax.broadcasted_iota(jnp.int32, (128, 128), 0)
    lane_of = lax.broadcasted_iota(jnp.int32, (128, 128), 1)
    pick = ((lane_of == first + row_of) & (row_of < held)).astype(BF16)
    nt = (((1,), (1,)), ((), ()))
    g = lax.dot_general(gates, pick, nt, preferred_element_type=F32)
    gt = lax.dot_general(pick, gates, nt, preferred_element_type=F32)
    up_t = lax.broadcasted_iota(jnp.int32, (tokens, tokens), 0)
    up_u = lax.broadcasted_iota(jnp.int32, (tokens, tokens), 1)
    before = jnp.where(up_t < up_u, 1.0, 0.0).astype(BF16)
    after_m = jnp.where(up_u < up_t, 1.0, 0.0).astype(BF16)
    on = jnp.where(g > 0, 1.0, 0.0).astype(BF16)
    ont = jnp.where(gt > 0, 1.0, 0.0).astype(BF16)
    rank = jnp.dot(after_m, on, preferred_element_type=F32)
    rankt = jnp.dot(ont, before, preferred_element_type=F32)
    rank = jnp.where(g > 0, rank, -1.0)
    gts[...] = jnp.where(gt > 0, rankt, -1.0)
    slot_lane = lax.broadcasted_iota(jnp.int32, (tokens, cap), 1).astype(F32)
    for h in range(held):
        col = jnp.where(rank[:, h : h + 1] == slot_lane, g[:, h : h + 1], 0.0).astype(BF16)
        cmat[:, :, h * cap : (h + 1) * cap] = col.reshape(2 * ys, zs * rows, cap)

    slot_row = lax.broadcasted_iota(jnp.int32, (cap, tokens), 0).astype(F32)

    def expert(h, carry):
        slot = h % slots
        sel = jnp.where(gts[pl.ds(h, 1), :] == slot_row, 1.0, 0.0).astype(BF16)
        for k in range(chunks):
            cols = slice(k * cw, (k + 1) * cw)
            xs[:, cols] = jnp.dot(
                sel, buf[:, :, cols].reshape(tokens, cw), preferred_element_type=F32
            ).astype(BF16)
        for cp in load_gu(h, slot):
            cp.wait()
        gated = jnp.dot(xs[...], wg[slot], preferred_element_type=F32)
        lifted = jnp.dot(xs[...], wu[slot], preferred_element_type=F32)
        act[h] = (gated / (1.0 + jnp.exp(-gated)) * lifted).astype(BF16)

        @pl.when(h + slots < held)
        def _():
            for cp in load_gu(h + slots, slot):
                cp.start()

        return carry

    lax.fori_loop(0, held, expert, 0)

    def produce(k):
        ks = k % dslots
        load_d(k).wait()

        def down(h, carry):
            at = pl.ds(pl.multiple_of(h * cap, cap), cap)
            ybuf[at, :] = jnp.dot(act[h], wd[ks, h], preferred_element_type=F32).astype(BF16)
            return carry

        lax.fori_loop(0, held, down, 0)
        if k + dslots < chunks:
            load_d(k + dslots).start()

        def mix(i):
            v = jnp.dot(cmat[i], ybuf[...], preferred_element_type=F32).astype(BF16)
            pbuf[k, pl.ds(i * zs, zs)] = v.reshape(zs, rows, cw)

        for e in [*range(1, ys), 0]:
            i = at_y(e) * 2 + t
            mix(i)
            cp = remote(pbuf.at[k, pl.ds(i * zs, zs)], trecv.at[k, e], rt_s.at[k, e], rt_r.at[k, e], twin, z)
            cp.start()
            pending.append(cp)
        for e in [*range(1, ys), 0]:
            mix(at_y(e) * 2 + c)

    def sum_twin(k):
        for e in [*range(1, ys), 0]:
            remote(trecv.at[k, e], trecv.at[k, e], rt_s.at[k, e], rt_r.at[k, e], twin, z).wait_recv()
            i = at_y(e) * 2 + c
            mine = pbuf[k, pl.ds(i * zs, zs)].astype(F32)
            ysend[k, e] = (mine + trecv[k, e].astype(F32)).astype(BF16)
            if e > 0:
                cp = remote(ysend.at[k, e], yrecv.at[k, ys - e], ry_s.at[k, e], ry_r.at[k, ys - e], at_y(e) * 2 + c, z)
                cp.start()
                pending.append(cp)

    def sum_y(k):
        total = ysend[k, 0].astype(F32)
        for e in range(1, ys):
            remote(yrecv.at[k, e], yrecv.at[k, e], ry_s.at[k, e], ry_r.at[k, e], at_y(e) * 2 + c, z).wait_recv()
            total = total + yrecv[k, e].astype(F32)
        zsend[k] = total.astype(BF16)
        for d in range(1, zs):
            zz = (z + d) % zs
            cp = remote(zsend.at[k, zz], zrecv.at[k, zs - d], rz_s.at[k, d], rz_r.at[k, zs - d], head, zz)
            cp.start()
            pending.append(cp)

    def finish(k):
        total = zsend[k, z].astype(F32)
        for d in range(1, zs):
            zz = (z + d) % zs
            remote(zsend.at[k, zz], zrecv.at[k, d], rz_s.at[k, d], rz_r.at[k, d], head, zz).wait_recv()
            total = total + zrecv[k, d].astype(F32)
        cols = slice(k * cw, (k + 1) * cw)
        out[:, cols] = (am[:, cols].astype(F32) + total).astype(BF16)

    for k in range(chunks):
        produce(k)
        if k >= 1:
            sum_twin(k - 1)
        if k >= 3:
            sum_y(k - 3)
    sum_twin(chunks - 1)
    for k in range(max(chunks - 3, 0), chunks):
        sum_y(k)
    for k in range(chunks):
        finish(k)
    for cp in pending:
        cp.wait_send()


def experts_block(mixed, residual, norm_gain, router, ids, gate_proj, up_proj, down_proj, capacity):
    heads = lax.axis_size("head")
    zs = lax.axis_size("req")
    ys = heads // 2
    rows, width = residual.shape
    held, _, hidden = gate_proj.shape
    chunks = 4
    slots = min(3, held)
    dslots = 2
    cw = width // chunks
    blocks = heads * zs
    tokens = blocks * rows
    cap = capacity * blocks
    vmem = pl.BlockSpec(memory_space=pltpu.VMEM)
    hbm = pl.BlockSpec(memory_space=pl.ANY)
    dma = pltpu.SemaphoreType.DMA
    return pl.pallas_call(
        functools.partial(block_kernel, ys, zs, cap, chunks),
        out_shape=jax.ShapeDtypeStruct((rows, width), BF16),
        in_specs=[vmem] * 5 + [hbm] * 3,
        out_specs=vmem,
        scratch_shapes=[
            pltpu.VMEM((blocks, rows, width + 128), BF16),
            pltpu.VMEM((slots, width, hidden), BF16),
            pltpu.VMEM((slots, width, hidden), BF16),
            pltpu.VMEM((dslots, held, hidden, cw), BF16),
            pltpu.VMEM((cap, width), BF16),
            pltpu.VMEM((held, cap, hidden), BF16),
            pltpu.VMEM((heads, zs * rows, held * cap), BF16),
            pltpu.VMEM((128, tokens), F32),
            pltpu.VMEM((held * cap, cw), BF16),
            pltpu.VMEM((chunks, blocks, rows, cw), BF16),
            pltpu.VMEM((chunks, ys, zs, rows, cw), BF16),
            pltpu.VMEM((chunks, ys, zs, rows, cw), BF16),
            pltpu.VMEM((chunks, ys, zs, rows, cw), BF16),
            pltpu.VMEM((chunks, zs, rows, cw), BF16),
            pltpu.VMEM((chunks, zs, rows, cw), BF16),
            pltpu.VMEM((ys, rows, width), F32),
            pltpu.VMEM((ys, rows, width), BF16),
            pltpu.VMEM((ys, rows, width), BF16),
            pltpu.VMEM((rows, width), BF16),
            dma((ys,)), dma((ys,)), dma((ys,)), dma((ys,)),
            dma((zs,)), dma((ys * zs,)), dma((ys * zs,)), dma((blocks,)),
            dma((chunks, ys)), dma((chunks, ys)), dma((chunks, ys)), dma((chunks, ys)),
            dma((chunks, zs)), dma((chunks, zs)),
            dma((slots, 2)), dma((dslots,)),
        ],
        compiler_params=pltpu.CompilerParams(
            collective_id=0, has_side_effects=True, vmem_limit_bytes=62 * 2**20
        ),
    )(
        mixed.reshape(ys, 2, rows, width), residual, norm_gain.reshape(1, width), router, ids,
        gate_proj, up_proj, down_proj,
    )


def body(
    ssm_input,
    write_vec,
    read_vec,
    step_raw,
    step_bias,
    decay_rate,
    skip_gain,
    cache_state,
    parents,
    out_proj,
    residual,
    norm_gain,
    router,
    expert_ids,
    gate_proj,
    up_proj,
    down_proj,
):
    nodes, requests, columns = ssm_input.shape
    heads = step_raw.shape[2]
    head_size = columns // heads
    state = write_vec.shape[2]
    both = lax.all_gather(jnp.concatenate([write_vec, read_vec], axis=2), "head", axis=0, tiled=True)
    writes, reads = both[:, :, :state], both[:, :, state:]
    inputs4 = ssm_input.reshape(nodes, requests, heads, head_size)
    step = jax.nn.softplus(step_raw + step_bias)
    rates = -step * decay_rate
    reach = ancestry(parents)
    depth = jnp.einsum("rji,irh->jrh", reach, rates, precision=lax.Precision.HIGHEST)
    affinity = jnp.einsum("jrn,irn->rji", reads, writes, preferred_element_type=jnp.float32)
    by_request = depth.transpose(1, 0, 2)
    spread = by_request[:, :, None, :] - by_request[:, None, :, :]
    linked = reach[:, :, :, None] > 0
    factor = jnp.where(linked, jnp.exp(jnp.where(linked, spread, 0.0)), 0.0)
    weights = (factor * affinity[:, :, :, None] * step.transpose(1, 0, 2)[:, None, :, :]).astype(
        jnp.bfloat16
    )
    tree_part = jnp.einsum("rjih,irhp->jrhp", weights, inputs4, preferred_element_type=jnp.float32)
    cache_part = jnp.einsum(
        "jrn,rhpn->jrhp", reads, cache_state, preferred_element_type=jnp.float32
    )
    cache_part = cache_part * jnp.exp(depth)[:, :, :, None]
    ssm_out = (tree_part + cache_part + skip_gain[:, None] * inputs4.astype(jnp.float32)).astype(
        jnp.bfloat16
    )
    ssm_out = ssm_out.reshape(nodes, requests, columns)
    local_nodes = residual.shape[0]
    width = residual.shape[2]
    mixed = jnp.einsum("jrk,kd->jrd", ssm_out, out_proj, preferred_element_type=jnp.float32)
    token_count = local_nodes * requests
    experts = router.shape[1]
    topk = expert_ids.shape[2]
    capacity = 2 * token_count * topk // (experts + experts // 4)
    layer_out = experts_block(
        mixed,
        residual.reshape(token_count, width),
        norm_gain,
        router,
        expert_ids.reshape(token_count, topk),
        gate_proj,
        up_proj,
        down_proj,
        capacity,
    )
    return layer_out.reshape(local_nodes, requests, width)


def solution(mesh):
    in_specs = (
        P(None, ("groups", "req"), "head"),
        P("head", ("groups", "req"), None),
        P("head", ("groups", "req"), None),
        P(None, ("groups", "req"), "head"),
        P("head"),
        P("head"),
        P("head"),
        P(("groups", "req"), "head", None, None),
        P(("groups", "req"), None),
        P("head", None),
        P("head", ("groups", "req"), None),
        P(),
        P(),
        P("head", ("groups", "req"), None),
        P(("head", "req"), None, None),
        P(("head", "req"), None, None),
        P(("head", "req"), None, None),
    )
    out_specs = P("head", ("groups", "req"), None)
    return jax.shard_map(body, mesh=mesh, in_specs=in_specs, out_specs=out_specs, check_vma=False)
```

```python
import functools
import jax
import jax.numpy as jnp
from jax import lax
from jax.experimental import pallas as pl
from jax.experimental.pallas import tpu as pltpu
from jax.sharding import PartitionSpec as P

F32 = jnp.float32
BF16 = jnp.bfloat16


def ancestry(parents):
    nodes = parents.shape[1]
    labels = jnp.arange(nodes, dtype=jnp.int32)
    power = (parents[:, :, None] == labels[None, None, :]).astype(BF16)
    reach = power + jnp.eye(nodes, dtype=BF16)
    covered = 2
    while covered < nodes:
        power = jnp.einsum("rjk,rki->rji", power, power, preferred_element_type=F32).astype(BF16)
        reach = reach + jnp.einsum("rjk,rki->rji", power, reach, preferred_element_type=F32).astype(BF16)
        covered *= 2
    return reach.astype(F32)


def remote(src, dst, send, recv, head, req):
    return pltpu.make_async_remote_copy(
        src_ref=src,
        dst_ref=dst,
        send_sem=send,
        recv_sem=recv,
        device_id={"head": head, "req": req},
        device_id_type=pl.DeviceIdType.MESH,
    )


def block_kernel(
    ys, zs, cap, chunks,
    part, res, gain, router, ids, wg_h, wu_h, wd_h,
    out,
    buf0, bufn, wg, wu, wd, smat, acc, act, cmat, ybuf, pbuf, trecv, ysend, yrecv, zsend, zrecv, mt, ms, my, am,
    mt_s, mt_r, my_s, my_r, az_s, ay_s, at_s, ar, rt_s, rt_r, ry_s, ry_r, rz_s, rz_r, w_s, d_s,
):
    head = lax.axis_index("head")
    z = lax.axis_index("req")
    y = head // 2
    c = head % 2
    t = 1 - c
    twin = y * 2 + t
    rows, width = res.shape
    experts = router.shape[0]
    held, hidden = wg_h.shape[0], wg_h.shape[2]
    slots = wg.shape[0]
    dslots = wd.shape[0]
    tokens = 2 * ys * zs * rows
    cw = width // chunks

    def at_y(d):
        return (y + d) % ys

    flip = 1 - 2 * (2 * z // zs)

    def at_z(d):
        return (z + flip * d + zs) % zs

    def blk(yy, cc, zz):
        return (yy * 2 + cc) * zs + zz

    units = held * chunks

    def load_gu(u):
        slot = u % slots
        at = pl.ds(pl.multiple_of((u // held) * cw, cw), cw)
        return (
            pltpu.make_async_copy(wg_h.at[u % held, at, :], wg.at[slot], w_s.at[slot, 0]),
            pltpu.make_async_copy(wu_h.at[u % held, at, :], wu.at[slot], w_s.at[slot, 1]),
        )

    def load_d(k):
        return pltpu.make_async_copy(
            wd_h.at[:, :, pl.ds(k * cw, cw)], wd.at[k % dslots], d_s.at[k % dslots]
        )

    barrier = pltpu.get_barrier_semaphore()
    pl.semaphore_signal(barrier, inc=1, device_id={"head": twin, "req": z}, device_id_type=pl.DeviceIdType.MESH)
    for d in range(1, ys):
        pl.semaphore_signal(barrier, inc=1, device_id={"head": at_y(d) * 2 + c, "req": z}, device_id_type=pl.DeviceIdType.MESH)
    for d in range(1, zs):
        pl.semaphore_signal(barrier, inc=1, device_id={"head": head, "req": (z + d) % zs}, device_id_type=pl.DeviceIdType.MESH)
    pl.semaphore_wait(barrier, ys + zs - 1)

    pending = []
    twin_parts = []
    for d in [*range(1, ys), 0]:
        cp = remote(part.at[at_y(d), t], mt.at[d], mt_s.at[d], mt_r.at[d], twin, z)
        cp.start()
        twin_parts.append((d, cp))
    for u in range(slots):
        for cp in load_gu(jnp.int32(u)):
            cp.start()
    for k in range(dslots):
        load_d(k).start()
    for d, cp in twin_parts:
        cp.wait_recv()
        if d > 0:
            ms[d] = (part[at_y(d), c] + mt[d]).astype(BF16)
            yc = remote(ms.at[d], my.at[ys - d], my_s.at[d], my_r.at[ys - d], at_y(d) * 2 + c, z)
            yc.start()
            pending.append(yc)
        pending.append(cp)
    mixed = part[y, c] + mt[0]
    for r in range(1, ys):
        remote(ms.at[r], my.at[r], my_s.at[r], my_r.at[r], at_y(r) * 2 + c, z).wait_recv()
        mixed = mixed + my[r].astype(F32)
    after = (res[...].astype(F32) + mixed).astype(BF16)
    am[...] = after
    wide = after.astype(F32)
    meansq = jnp.mean(wide * wide, axis=-1, keepdims=True)
    normed = (wide * lax.rsqrt(meansq + 1e-05) * gain[...]).astype(BF16)
    own = blk(y, c, z)
    nt = (((1,), (1,)), ((), ()))
    buf0[own, :, :cw] = normed[:, :cw]
    for k in range(1, chunks):
        bufn[k - 1, own] = normed[:, k * cw : (k + 1) * cw]
    logits = lax.dot_general(normed, router[...], nt, preferred_element_type=F32)
    lanes = lax.broadcasted_iota(jnp.int32, (rows, experts), 1)
    chosen = ids[...]
    named = lanes == chosen[:, 0:1]
    for k in range(1, ids.shape[1]):
        named = named | (lanes == chosen[:, k : k + 1])
    powered = jnp.where(named, jnp.exp(jnp.where(named, logits, 0.0)), 0.0)
    gate = powered / jnp.sum(powered, axis=1, keepdims=True)
    if experts < 128:
        gate = jnp.concatenate([gate, jnp.zeros((rows, 128 - experts), F32)], axis=1)
    buf0[own, :, cw:] = gate.astype(BF16)

    def block(k, b):
        return buf0.at[b] if k == 0 else bufn.at[k - 1, b]

    def pass_y(k, b, i):
        for d in range(1, ys):
            s = (d - 1) * zs + i
            cp = remote(block(k, b), block(k, b), ay_s.at[k, s], ar.at[k, b], at_y(d) * 2 + c, z)
            cp.start()
            pending.append(cp)

    def pass_twin(k, b, i):
        cp = remote(block(k, b), block(k, b), at_s.at[k, i], ar.at[k, b], twin, z)
        cp.start()
        pending.append(cp)

    def landed(k, b):
        remote(block(k, b), block(k, b), at_s.at[k, 0], ar.at[k, b], twin, z).wait_recv()

    def send_own(k):
        pass_y(k, own, 0)
        for d in range(1, zs):
            cp = remote(block(k, own), block(k, own), az_s.at[k, d], ar.at[k, own], head, at_z(d))
            cp.start()
            pending.append(cp)
        pass_twin(k, own, 0)

    def relay_z(k):
        for d in range(1, zs):
            b = blk(y, c, at_z(d))
            landed(k, b)
            pass_y(k, b, d)
            pass_twin(k, b, d)

    def relay_y(k):
        for e in range(1, ys):
            for d in range(zs):
                b = blk(at_y(e), c, at_z(d))
                landed(k, b)
                pass_twin(k, b, e * zs + d)

    def all_in(k):
        for e in range(ys):
            for d in range(zs):
                landed(k, blk(at_y(e), t, at_z(d)))

    def select(k):
        rows_k = (buf0[:, :, :cw] if k == 0 else bufn[k - 1]).reshape(tokens, cw)
        half = cw // 2
        for n in range(2):
            cols = slice(n * half, (n + 1) * half)
            ybuf[:, cols] = jnp.dot(smat[...], rows_k[:, cols], preferred_element_type=F32).astype(BF16)

    def apply(k, low, high):
        def expert(h, carry):
            u = k * held + h
            slot = u % slots
            x = ybuf[pl.ds(pl.multiple_of(h * cap, cap), cap), :]
            for cp in load_gu(u):
                cp.wait()
            gated = jnp.dot(x, wg[slot], preferred_element_type=F32)
            lifted = jnp.dot(x, wu[slot], preferred_element_type=F32)
            if k > 0:
                gated = gated + acc[h, 0]
                lifted = lifted + acc[h, 1]
            if k < chunks - 1:
                acc[h, 0] = gated
                acc[h, 1] = lifted
            else:
                act[h] = (gated / (1.0 + jnp.exp(-gated)) * lifted).astype(BF16)

            @pl.when(u + slots < units)
            def _():
                for cp in load_gu(u + slots):
                    cp.start()

            return carry

        lax.fori_loop(low, high, expert, 0)

    for k in range(chunks):
        send_own(k)
    relay_z(0)
    relay_y(0)
    all_in(0)

    gates = buf0[:, :, cw:].reshape(tokens, 128)
    first = ((head * zs + z) * held) % experts
    row_of = lax.broadcasted_iota(jnp.int32, (128, 128), 0)
    lane_of = lax.broadcasted_iota(jnp.int32, (128, 128), 1)
    pick = ((lane_of == first + row_of) & (row_of < held)).astype(BF16)
    g = lax.dot_general(gates, pick, nt, preferred_element_type=F32)
    gt = lax.dot_general(pick, gates, nt, preferred_element_type=F32)
    up_t = lax.broadcasted_iota(jnp.int32, (tokens, tokens), 0)
    up_u = lax.broadcasted_iota(jnp.int32, (tokens, tokens), 1)
    before = jnp.where(up_t < up_u, 1.0, 0.0).astype(BF16)
    after_m = jnp.where(up_u < up_t, 1.0, 0.0).astype(BF16)
    on = jnp.where(g > 0, 1.0, 0.0).astype(BF16)
    ont = jnp.where(gt > 0, 1.0, 0.0).astype(BF16)
    rank = jnp.dot(after_m, on, preferred_element_type=F32)
    rankt = jnp.dot(ont, before, preferred_element_type=F32)
    rank = jnp.where(g > 0, rank, -1.0)
    rankt = jnp.where(gt > 0, rankt, -1.0)
    slot_row = lax.broadcasted_iota(jnp.int32, (cap, tokens), 0).astype(F32)
    for h in range(held):
        smat[h * cap : (h + 1) * cap, :] = jnp.where(rankt[h : h + 1, :] == slot_row, 1.0, 0.0).astype(BF16)
    select(0)
    relay_z(1)
    slot_lane = lax.broadcasted_iota(jnp.int32, (tokens, cap), 1).astype(F32)
    for h in range(held):
        col = jnp.where(rank[:, h : h + 1] == slot_lane, g[:, h : h + 1], 0.0).astype(BF16)
        col = col.reshape(ys, 2, zs * rows, cap)
        for e in range(ys):
            for cc in range(2):
                cmat[cc, e * zs * rows : (e + 1) * zs * rows, h * cap : (h + 1) * cap] = col[e, cc]

    middle = held // 2
    for k in range(chunks):
        if k > 0:
            select(k)
        apply(k, 0, middle)
        if k + 1 < chunks:
            relay_y(k + 1)
        apply(k, middle, held)
        if k + 2 < chunks:
            relay_z(k + 2)
        if k + 1 < chunks:
            all_in(k + 1)

    def produce(k):
        ks = k % dslots
        load_d(k).wait()

        def down(h, carry):
            at = pl.ds(pl.multiple_of(h * cap, cap), cap)
            ybuf[at, :] = jnp.dot(act[h], wd[ks, h], preferred_element_type=F32).astype(BF16)
            return carry

        lax.fori_loop(0, held, down, 0)
        if k + dslots < chunks:
            load_d(k + dslots).start()

        def mix(cc):
            v = jnp.dot(cmat[cc], ybuf[...], preferred_element_type=F32).astype(BF16)
            pbuf[k, cc] = v.reshape(ys, zs, rows, cw)

        mix(t)
        for e in [*range(1, ys), 0]:
            cp = remote(pbuf.at[k, t, at_y(e)], trecv.at[k, e], rt_s.at[k, e], rt_r.at[k, e], twin, z)
            cp.start()
            pending.append(cp)
        mix(c)

    def sum_twin(k):
        for e in [*range(1, ys), 0]:
            remote(trecv.at[k, e], trecv.at[k, e], rt_s.at[k, e], rt_r.at[k, e], twin, z).wait_recv()
            mine = pbuf[k, c, at_y(e)].astype(F32)
            ysend[k, e] = (mine + trecv[k, e].astype(F32)).astype(BF16)
            if e > 0:
                cp = remote(ysend.at[k, e], yrecv.at[k, ys - e], ry_s.at[k, e], ry_r.at[k, ys - e], at_y(e) * 2 + c, z)
                cp.start()
                pending.append(cp)

    def sum_y(k):
        total = ysend[k, 0].astype(F32)
        for e in range(1, ys):
            remote(yrecv.at[k, e], yrecv.at[k, e], ry_s.at[k, e], ry_r.at[k, e], at_y(e) * 2 + c, z).wait_recv()
            total = total + yrecv[k, e].astype(F32)
        zsend[k] = total.astype(BF16)
        for d in range(1, zs):
            zz = (z + d) % zs
            cp = remote(zsend.at[k, zz], zrecv.at[k, zs - d], rz_s.at[k, d], rz_r.at[k, zs - d], head, zz)
            cp.start()
            pending.append(cp)

    def finish(k):
        total = zsend[k, z].astype(F32)
        for d in range(1, zs):
            zz = (z + d) % zs
            remote(zsend.at[k, zz], zrecv.at[k, d], rz_s.at[k, d], rz_r.at[k, d], head, zz).wait_recv()
            total = total + zrecv[k, d].astype(F32)
        cols = slice(k * cw, (k + 1) * cw)
        out[:, cols] = (am[:, cols].astype(F32) + total).astype(BF16)

    for k in range(chunks):
        produce(k)
        if k >= 1:
            sum_twin(k - 1)
        if k >= 3:
            sum_y(k - 3)
    sum_twin(chunks - 1)
    for k in range(max(chunks - 3, 0), chunks):
        sum_y(k)
    for k in range(chunks):
        finish(k)
    for cp in pending:
        cp.wait_send()


def experts_block(mixed, residual, norm_gain, router, ids, gate_proj, up_proj, down_proj, capacity):
    heads = lax.axis_size("head")
    zs = lax.axis_size("req")
    ys = heads // 2
    rows, width = residual.shape
    held, _, hidden = gate_proj.shape
    chunks = 4
    slots = min(12, held * 4)
    dslots = 2
    cw = width // chunks
    blocks = heads * zs
    tokens = blocks * rows
    cap = capacity * blocks
    vmem = pl.BlockSpec(memory_space=pltpu.VMEM)
    hbm = pl.BlockSpec(memory_space=pl.ANY)
    dma = pltpu.SemaphoreType.DMA
    return pl.pallas_call(
        functools.partial(block_kernel, ys, zs, cap, chunks),
        out_shape=jax.ShapeDtypeStruct((rows, width), BF16),
        in_specs=[vmem] * 5 + [hbm] * 3,
        out_specs=vmem,
        scratch_shapes=[
            pltpu.VMEM((blocks, rows, cw + 128), BF16),
            pltpu.VMEM((chunks - 1, blocks, rows, cw), BF16),
            pltpu.VMEM((slots, cw, hidden), BF16),
            pltpu.VMEM((slots, cw, hidden), BF16),
            pltpu.VMEM((dslots, held, hidden, cw), BF16),
            pltpu.VMEM((held * cap, tokens), BF16),
            pltpu.VMEM((held, 2, cap, hidden), F32),
            pltpu.VMEM((held, cap, hidden), BF16),
            pltpu.VMEM((2, ys * zs * rows, held * cap), BF16),
            pltpu.VMEM((held * cap, cw), BF16),
            pltpu.VMEM((chunks, 2, ys, zs, rows, cw), BF16),
            pltpu.VMEM((chunks, ys, zs, rows, cw), BF16),
            pltpu.VMEM((chunks, ys, zs, rows, cw), BF16),
            pltpu.VMEM((chunks, ys, zs, rows, cw), BF16),
            pltpu.VMEM((chunks, zs, rows, cw), BF16),
            pltpu.VMEM((chunks, zs, rows, cw), BF16),
            pltpu.VMEM((ys, rows, width), F32),
            pltpu.VMEM((ys, rows, width), BF16),
            pltpu.VMEM((ys, rows, width), BF16),
            pltpu.VMEM((rows, width), BF16),
            dma((ys,)), dma((ys,)), dma((ys,)), dma((ys,)),
            dma((chunks, zs)), dma((chunks, ys * zs)), dma((chunks, ys * zs)), dma((chunks, blocks)),
            dma((chunks, ys)), dma((chunks, ys)), dma((chunks, ys)), dma((chunks, ys)),
            dma((chunks, zs)), dma((chunks, zs)),
            dma((slots, 2)), dma((dslots,)),
        ],
        compiler_params=pltpu.CompilerParams(
            collective_id=0, has_side_effects=True, vmem_limit_bytes=62 * 2**20
        ),
    )(
        mixed.reshape(ys, 2, rows, width), residual, norm_gain.reshape(1, width), router.T, ids,
        gate_proj, up_proj, down_proj,
    )


def body(
    ssm_input,
    write_vec,
    read_vec,
    step_raw,
    step_bias,
    decay_rate,
    skip_gain,
    cache_state,
    parents,
    out_proj,
    residual,
    norm_gain,
    router,
    expert_ids,
    gate_proj,
    up_proj,
    down_proj,
):
    nodes, requests, columns = ssm_input.shape
    heads = step_raw.shape[2]
    head_size = columns // heads
    state = write_vec.shape[2]
    both = lax.all_gather(jnp.concatenate([write_vec, read_vec], axis=2), "head", axis=0, tiled=True)
    writes, reads = both[:, :, :state], both[:, :, state:]
    inputs4 = ssm_input.reshape(nodes, requests, heads, head_size)
    step = jax.nn.softplus(step_raw + step_bias)
    rates = -step * decay_rate
    reach = ancestry(parents)
    depth = jnp.einsum("rji,irh->jrh", reach, rates, precision=lax.Precision.HIGHEST)
    affinity = jnp.einsum("jrn,irn->rji", reads, writes, preferred_element_type=jnp.float32)
    by_request = depth.transpose(1, 0, 2)
    spread = by_request[:, :, None, :] - by_request[:, None, :, :]
    linked = reach[:, :, :, None] > 0
    factor = jnp.where(linked, jnp.exp(jnp.where(linked, spread, 0.0)), 0.0)
    weights = (factor * affinity[:, :, :, None] * step.transpose(1, 0, 2)[:, None, :, :]).astype(
        jnp.bfloat16
    )
    tree_part = jnp.einsum("rjih,irhp->jrhp", weights, inputs4, preferred_element_type=jnp.float32)
    cache_part = jnp.einsum(
        "jrn,rhpn->jrhp", reads, cache_state, preferred_element_type=jnp.float32
    )
    cache_part = cache_part * jnp.exp(depth)[:, :, :, None]
    ssm_out = (tree_part + cache_part + skip_gain[:, None] * inputs4.astype(jnp.float32)).astype(
        jnp.bfloat16
    )
    ssm_out = ssm_out.reshape(nodes, requests, columns)
    local_nodes = residual.shape[0]
    width = residual.shape[2]
    mixed = jnp.einsum("jrk,kd->jrd", ssm_out, out_proj, preferred_element_type=jnp.float32)
    token_count = local_nodes * requests
    experts = router.shape[1]
    topk = expert_ids.shape[2]
    capacity = 2 * token_count * topk // (experts + experts // 4)
    layer_out = experts_block(
        mixed,
        residual.reshape(token_count, width),
        norm_gain,
        router,
        expert_ids.reshape(token_count, topk),
        gate_proj,
        up_proj,
        down_proj,
        capacity,
    )
    return layer_out.reshape(local_nodes, requests, width)


def solution(mesh):
    in_specs = (
        P(None, ("groups", "req"), "head"),
        P("head", ("groups", "req"), None),
        P("head", ("groups", "req"), None),
        P(None, ("groups", "req"), "head"),
        P("head"),
        P("head"),
        P("head"),
        P(("groups", "req"), "head", None, None),
        P(("groups", "req"), None),
        P("head", None),
        P("head", ("groups", "req"), None),
        P(),
        P(),
        P("head", ("groups", "req"), None),
        P(("head", "req"), None, None),
        P(("head", "req"), None, None),
        P(("head", "req"), None, None),
    )
    out_specs = P("head", ("groups", "req"), None)
    return jax.shard_map(body, mesh=mesh, in_specs=in_specs, out_specs=out_specs, check_vma=False)
```

```python
import functools
import jax
import jax.numpy as jnp
from jax import lax
from jax.experimental import pallas as pl
from jax.experimental.pallas import tpu as pltpu
from jax.sharding import PartitionSpec as P

F32 = jnp.float32
BF16 = jnp.bfloat16


def ancestry(parents):
    nodes = parents.shape[1]
    labels = jnp.arange(nodes, dtype=jnp.int32)
    power = (parents[:, :, None] == labels[None, None, :]).astype(BF16)
    reach = power + jnp.eye(nodes, dtype=BF16)
    covered = 2
    while covered < nodes:
        power = jnp.einsum("rjk,rki->rji", power, power, preferred_element_type=F32).astype(BF16)
        reach = reach + jnp.einsum("rjk,rki->rji", power, reach, preferred_element_type=F32).astype(BF16)
        covered *= 2
    return reach.astype(F32)


def remote(src, dst, send, recv, head, req):
    return pltpu.make_async_remote_copy(
        src_ref=src,
        dst_ref=dst,
        send_sem=send,
        recv_sem=recv,
        device_id={"head": head, "req": req},
        device_id_type=pl.DeviceIdType.MESH,
    )


def block_kernel(
    ys, zs, cap, chunks, backs,
    ssm, proj_h, res, gain, router, ids, wg_h, wu_h, wd_h,
    out,
    part, proj, buf0, bufn, wgu, wd, smat, acc, act, cmat, ybuf, pbuf, trecv, ysend, yrecv, zsend, zrecv, mt, ms, my, am,
    p_s, mt_s, mt_r, my_s, my_r, az_s, ay_s, at_s, ar, atr, rt_s, rt_r, ry_s, ry_r, rz_s, rz_r, w_s, d_s,
):
    head = lax.axis_index("head")
    z = lax.axis_index("req")
    y = head // 2
    c = head % 2
    t = 1 - c
    twin = y * 2 + t
    rows, width = res.shape
    experts = router.shape[0]
    held, hidden = wg_h.shape[0], wg_h.shape[2]
    slots = wgu.shape[0]
    dslots = wd.shape[0]
    tokens = 2 * ys * zs * rows
    cw = width // chunks
    rw = width // backs

    def at_y(d):
        return (y + d) % ys

    flip = 1 - 2 * (2 * z // zs)

    def at_z(d):
        return (z + flip * d + zs) % zs

    def blk(yy, cc, zz):
        return (yy * 2 + cc) * zs + zz

    units = held * chunks

    def load_gu(u):
        slot = u % slots
        at = pl.ds(pl.multiple_of((u // held) * cw, cw), cw)
        return (
            pltpu.make_async_copy(wg_h.at[u % held, at, :], wgu.at[slot, :, pl.ds(0, hidden)], w_s.at[slot, 0]),
            pltpu.make_async_copy(wu_h.at[u % held, at, :], wgu.at[slot, :, pl.ds(hidden, hidden)], w_s.at[slot, 1]),
        )

    def load_d(k):
        return pltpu.make_async_copy(
            wd_h.at[:, :, pl.ds(k * rw, rw)], wd.at[k % dslots], d_s.at[k % dslots]
        )

    def load_p(k):
        return pltpu.make_async_copy(proj_h.at[:, pl.ds(k * cw, cw)], proj.at[k % 2], p_s.at[k % 2])

    load_p(0).start()
    load_p(1).start()
    for u in range(slots):
        for cp in load_gu(jnp.int32(u)):
            cp.start()
    for k in range(dslots):
        load_d(k).start()

    barrier = pltpu.get_barrier_semaphore()
    pl.semaphore_signal(barrier, inc=1, device_id={"head": twin, "req": z}, device_id_type=pl.DeviceIdType.MESH)
    for d in range(1, ys):
        pl.semaphore_signal(barrier, inc=1, device_id={"head": at_y(d) * 2 + c, "req": z}, device_id_type=pl.DeviceIdType.MESH)
    for d in range(1, zs):
        pl.semaphore_signal(barrier, inc=1, device_id={"head": head, "req": (z + d) % zs}, device_id_type=pl.DeviceIdType.MESH)
    pl.semaphore_wait(barrier, ys + zs - 1)

    pending = []

    def mixer(k):
        load_p(k).wait()
        v = jnp.dot(ssm[...], proj[k % 2], preferred_element_type=F32)
        part[k] = v.reshape(ys, 2, rows, cw)
        if k + 2 < chunks:
            load_p(k + 2).start()
        for d in [*range(1, ys), 0]:
            cp = remote(part.at[k, at_y(d), t], mt.at[k, d], mt_s.at[k, d], mt_r.at[k, d], twin, z)
            cp.start()
            pending.append(cp)

    def mixer_y(k):
        for d in range(1, ys):
            remote(mt.at[k, d], mt.at[k, d], mt_s.at[k, d], mt_r.at[k, d], twin, z).wait_recv()
            ms[k, d] = (part[k, at_y(d), c] + mt[k, d]).astype(BF16)
            cp = remote(ms.at[k, d], my.at[k, ys - d], my_s.at[k, d], my_r.at[k, ys - d], at_y(d) * 2 + c, z)
            cp.start()
            pending.append(cp)

    for k in range(chunks):
        mixer(k)
        if k > 0:
            mixer_y(k - 1)
    mixer_y(chunks - 1)
    sums = []
    for k in range(chunks):
        remote(mt.at[k, 0], mt.at[k, 0], mt_s.at[k, 0], mt_r.at[k, 0], twin, z).wait_recv()
        total = part[k, y, c] + mt[k, 0]
        for r in range(1, ys):
            remote(ms.at[k, r], my.at[k, r], my_s.at[k, r], my_r.at[k, r], at_y(r) * 2 + c, z).wait_recv()
            total = total + my[k, r].astype(F32)
        sums.append(total)
    mixed = jnp.concatenate(sums, axis=1)
    after = (res[...].astype(F32) + mixed).astype(BF16)
    am[...] = after
    wide = after.astype(F32)
    meansq = jnp.mean(wide * wide, axis=-1, keepdims=True)
    normed = (wide * lax.rsqrt(meansq + 1e-05) * gain[...]).astype(BF16)
    own = blk(y, c, z)
    nt = (((1,), (1,)), ((), ()))
    buf0[own, :, :cw] = normed[:, :cw]
    for k in range(1, chunks):
        bufn[k - 1, own] = normed[:, k * cw : (k + 1) * cw]
    logits = lax.dot_general(normed, router[...], nt, preferred_element_type=F32)
    lanes = lax.broadcasted_iota(jnp.int32, (rows, experts), 1)
    chosen = ids[...]
    named = lanes == chosen[:, 0:1]
    for k in range(1, ids.shape[1]):
        named = named | (lanes == chosen[:, k : k + 1])
    powered = jnp.where(named, jnp.exp(jnp.where(named, logits, 0.0)), 0.0)
    gate = powered / jnp.sum(powered, axis=1, keepdims=True)
    if experts < 128:
        gate = jnp.concatenate([gate, jnp.zeros((rows, 128 - experts), F32)], axis=1)
    buf0[own, :, cw:] = gate.astype(BF16)

    def block(k, b):
        return buf0.at[b] if k == 0 else bufn.at[k - 1, b]

    def pass_y(k, b, i):
        for d in range(1, ys):
            s = (d - 1) * zs + i
            cp = remote(block(k, b), block(k, b), ay_s.at[k, s], ar.at[k, b], at_y(d) * 2 + c, z)
            cp.start()
            pending.append(cp)

    def pass_twin(k, e):
        at = pl.ds(blk(at_y(e), c, 0), zs)
        ref = buf0.at[at] if k == 0 else bufn.at[k - 1, at]
        cp = remote(ref, ref, at_s.at[k, e], atr.at[k, e], twin, z)
        cp.start()
        pending.append(cp)

    def landed(k, b):
        remote(block(k, b), block(k, b), at_s.at[k, 0], ar.at[k, b], twin, z).wait_recv()

    def send_z(k):
        for d in range(1, zs):
            cp = remote(block(k, own), block(k, own), az_s.at[k, d], ar.at[k, own], head, at_z(d))
            cp.start()
            pending.append(cp)

    def relay_z(k):
        for d in range(1, zs):
            b = blk(y, c, at_z(d))
            landed(k, b)
            pass_y(k, b, d)
        pass_twin(k, 0)
        if k + 2 < chunks:
            pass_y(k + 2, own, 0)

    def relay_y(k):
        for e in range(1, ys):
            for d in range(zs):
                landed(k, blk(at_y(e), c, at_z(d)))
            pass_twin(k, e)

    def all_in(k):
        for e in range(ys):
            at = pl.ds(blk(at_y(e), t, 0), zs)
            ref = buf0.at[at] if k == 0 else bufn.at[k - 1, at]
            remote(ref, ref, at_s.at[k, e], atr.at[k, e], twin, z).wait_recv()

    def select(k):
        rows_k = (buf0[:, :, :cw] if k == 0 else bufn[k - 1]).reshape(tokens, cw)
        half = cw // 2
        for n in range(2):
            cols = slice(n * half, (n + 1) * half)
            ybuf[:, cols] = jnp.dot(smat[...], rows_k[:, cols], preferred_element_type=F32).astype(BF16)

    def apply(k, low, high):
        def expert(h, carry):
            u = k * held + h
            slot = u % slots
            x = ybuf[pl.ds(pl.multiple_of(h * cap, cap), cap), :]
            for cp in load_gu(u):
                cp.wait()
            both = jnp.dot(x, wgu[slot], preferred_element_type=F32)
            if k > 0:
                both = both + acc[h]
            if k < chunks - 1:
                acc[h] = both
            else:
                gated = both[:, :hidden]
                act[h] = (gated / (1.0 + jnp.exp(-gated)) * both[:, hidden:]).astype(BF16)

            @pl.when(u + slots < units)
            def _():
                for cp in load_gu(u + slots):
                    cp.start()

            return carry

        lax.fori_loop(low, high, expert, 0)

    for k in range(chunks):
        if k < 2:
            pass_y(k, own, 0)
        send_z(k)
    relay_z(0)
    relay_y(0)
    all_in(0)

    gates = buf0[:, :, cw:].reshape(tokens, 128)
    first = ((head * zs + z) * held) % experts
    row_of = lax.broadcasted_iota(jnp.int32, (128, 128), 0)
    lane_of = lax.broadcasted_iota(jnp.int32, (128, 128), 1)
    pick = ((lane_of == first + row_of) & (row_of < held)).astype(BF16)
    g = lax.dot_general(gates, pick, nt, preferred_element_type=F32)
    gt = lax.dot_general(pick, gates, nt, preferred_element_type=F32)
    up_t = lax.broadcasted_iota(jnp.int32, (tokens, tokens), 0)
    up_u = lax.broadcasted_iota(jnp.int32, (tokens, tokens), 1)
    before = jnp.where(up_t < up_u, 1.0, 0.0).astype(BF16)
    after_m = jnp.where(up_u < up_t, 1.0, 0.0).astype(BF16)
    on = jnp.where(g > 0, 1.0, 0.0).astype(BF16)
    ont = jnp.where(gt > 0, 1.0, 0.0).astype(BF16)
    rank = jnp.dot(after_m, on, preferred_element_type=F32)
    rankt = jnp.dot(ont, before, preferred_element_type=F32)
    rank = jnp.where(g > 0, rank, -1.0)
    rankt = jnp.where(gt > 0, rankt, -1.0)
    slot_row = lax.broadcasted_iota(jnp.int32, (cap, tokens), 0).astype(F32)
    for h in range(held):
        smat[h * cap : (h + 1) * cap, :] = jnp.where(rankt[h : h + 1, :] == slot_row, 1.0, 0.0).astype(BF16)
    select(0)
    relay_z(1)
    slot_lane = lax.broadcasted_iota(jnp.int32, (tokens, cap), 1).astype(F32)
    for h in range(held):
        col = jnp.where(rank[:, h : h + 1] == slot_lane, g[:, h : h + 1], 0.0).astype(BF16)
        col = col.reshape(ys, 2, zs * rows, cap)
        for e in range(ys):
            for cc in range(2):
                cmat[cc, e * zs * rows : (e + 1) * zs * rows, h * cap : (h + 1) * cap] = col[e, cc]

    middle = held // 2
    for k in range(chunks):
        if k > 0:
            select(k)
        apply(k, 0, middle)
        if k + 1 < chunks:
            relay_y(k + 1)
        apply(k, middle, held)
        if k + 2 < chunks:
            relay_z(k + 2)
        if k + 1 < chunks:
            all_in(k + 1)

    def produce(k):
        ks = k % dslots
        load_d(k).wait()

        def down(h, carry):
            at = pl.ds(pl.multiple_of(h * cap, cap), cap)
            ybuf[at, :rw] = jnp.dot(act[h], wd[ks, h], preferred_element_type=F32).astype(BF16)
            return carry

        lax.fori_loop(0, held, down, 0)
        if k + dslots < backs:
            load_d(k + dslots).start()

        def mix(cc):
            v = jnp.dot(cmat[cc], ybuf[:, :rw], preferred_element_type=F32).astype(BF16)
            pbuf[k, cc] = v.reshape(ys, zs, rows, rw)

        mix(t)
        for e in [*range(1, ys), 0]:
            cp = remote(pbuf.at[k, t, at_y(e)], trecv.at[k, e], rt_s.at[k, e], rt_r.at[k, e], twin, z)
            cp.start()
            pending.append(cp)
        mix(c)

    def sum_twin(k):
        for e in [*range(1, ys), 0]:
            remote(trecv.at[k, e], trecv.at[k, e], rt_s.at[k, e], rt_r.at[k, e], twin, z).wait_recv()
            mine = pbuf[k, c, at_y(e)].astype(F32)
            ysend[k, e] = (mine + trecv[k, e].astype(F32)).astype(BF16)
            if e > 0:
                cp = remote(ysend.at[k, e], yrecv.at[k, ys - e], ry_s.at[k, e], ry_r.at[k, ys - e], at_y(e) * 2 + c, z)
                cp.start()
                pending.append(cp)

    def sum_y(k):
        total = ysend[k, 0].astype(F32)
        for e in range(1, ys):
            remote(yrecv.at[k, e], yrecv.at[k, e], ry_s.at[k, e], ry_r.at[k, e], at_y(e) * 2 + c, z).wait_recv()
            total = total + yrecv[k, e].astype(F32)
        zsend[k] = total.astype(BF16)
        for d in range(1, zs):
            zz = (z + d) % zs
            cp = remote(zsend.at[k, zz], zrecv.at[k, zs - d], rz_s.at[k, d], rz_r.at[k, zs - d], head, zz)
            cp.start()
            pending.append(cp)

    def finish(k):
        total = zsend[k, z].astype(F32)
        for d in range(1, zs):
            zz = (z + d) % zs
            remote(zsend.at[k, zz], zrecv.at[k, d], rz_s.at[k, d], rz_r.at[k, d], head, zz).wait_recv()
            total = total + zrecv[k, d].astype(F32)
        cols = slice(k * rw, (k + 1) * rw)
        out[:, cols] = (am[:, cols].astype(F32) + total).astype(BF16)

    for k in range(backs):
        produce(k)
        if k < 2:
            sum_twin(k)
        elif k > 2:
            sum_twin(k - 1)
        if k >= 4:
            sum_y(k - 4)
        if k >= 6:
            finish(k - 6)
    sum_twin(backs - 1)
    for k in range(backs - 4, backs):
        sum_y(k)
        finish(k - 2)
    finish(backs - 2)
    finish(backs - 1)
    for cp in pending:
        cp.wait_send()


def experts_block(ssm_out, out_proj, residual, norm_gain, router, ids, gate_proj, up_proj, down_proj, capacity):
    heads = lax.axis_size("head")
    zs = lax.axis_size("req")
    ys = heads // 2
    rows, width = residual.shape
    held, _, hidden = gate_proj.shape
    chunks = 4
    backs = 8
    slots = min(8, held * chunks)
    dslots = 4
    cw = width // chunks
    rw = width // backs
    blocks = heads * zs
    tokens = blocks * rows
    cap = capacity * blocks
    vmem = pl.BlockSpec(memory_space=pltpu.VMEM)
    hbm = pl.BlockSpec(memory_space=pl.ANY)
    dma = pltpu.SemaphoreType.DMA
    return pl.pallas_call(
        functools.partial(block_kernel, ys, zs, cap, chunks, backs),
        out_shape=jax.ShapeDtypeStruct((rows, width), BF16),
        in_specs=[vmem, hbm] + [vmem] * 4 + [hbm] * 3,
        out_specs=vmem,
        scratch_shapes=[
            pltpu.VMEM((chunks, ys, 2, rows, cw), F32),
            pltpu.VMEM((2, ssm_out.shape[1], cw), BF16),
            pltpu.VMEM((blocks, rows, cw + 128), BF16),
            pltpu.VMEM((chunks - 1, blocks, rows, cw), BF16),
            pltpu.VMEM((slots, cw, 2 * hidden), BF16),
            pltpu.VMEM((dslots, held, hidden, rw), BF16),
            pltpu.VMEM((held * cap, tokens), BF16),
            pltpu.VMEM((held, cap, 2 * hidden), F32),
            pltpu.VMEM((held, cap, hidden), BF16),
            pltpu.VMEM((2, ys * zs * rows, held * cap), BF16),
            pltpu.VMEM((held * cap, cw), BF16),
            pltpu.VMEM((backs, 2, ys, zs, rows, rw), BF16),
            pltpu.VMEM((backs, ys, zs, rows, rw), BF16),
            pltpu.VMEM((backs, ys, zs, rows, rw), BF16),
            pltpu.VMEM((backs, ys, zs, rows, rw), BF16),
            pltpu.VMEM((backs, zs, rows, rw), BF16),
            pltpu.VMEM((backs, zs, rows, rw), BF16),
            pltpu.VMEM((chunks, ys, rows, cw), F32),
            pltpu.VMEM((chunks, ys, rows, cw), BF16),
            pltpu.VMEM((chunks, ys, rows, cw), BF16),
            pltpu.VMEM((rows, width), BF16),
            dma((2,)), dma((chunks, ys)), dma((chunks, ys)), dma((chunks, ys)), dma((chunks, ys)),
            dma((chunks, zs)), dma((chunks, ys * zs)), dma((chunks, ys)), dma((chunks, blocks)), dma((chunks, ys)),
            dma((backs, ys)), dma((backs, ys)), dma((backs, ys)), dma((backs, ys)),
            dma((backs, zs)), dma((backs, zs)),
            dma((slots, 2)), dma((dslots,)),
        ],
        compiler_params=pltpu.CompilerParams(
            collective_id=0, has_side_effects=True, vmem_limit_bytes=62 * 2**20
        ),
    )(
        ssm_out, out_proj, residual, norm_gain.reshape(1, width), router.T, ids,
        gate_proj, up_proj, down_proj,
    )


def body(
    ssm_input,
    write_vec,
    read_vec,
    step_raw,
    step_bias,
    decay_rate,
    skip_gain,
    cache_state,
    parents,
    out_proj,
    residual,
    norm_gain,
    router,
    expert_ids,
    gate_proj,
    up_proj,
    down_proj,
):
    nodes, requests, columns = ssm_input.shape
    heads = step_raw.shape[2]
    head_size = columns // heads
    state = write_vec.shape[2]
    both = lax.all_gather(jnp.concatenate([write_vec, read_vec], axis=2), "head", axis=0, tiled=True)
    writes, reads = both[:, :, :state], both[:, :, state:]
    inputs4 = ssm_input.reshape(nodes, requests, heads, head_size)
    step = jax.nn.softplus(step_raw + step_bias)
    rates = -step * decay_rate
    reach = ancestry(parents)
    depth = jnp.einsum("rji,irh->jrh", reach, rates, precision=lax.Precision.HIGHEST)
    affinity = jnp.einsum("jrn,irn->rji", reads, writes, preferred_element_type=jnp.float32)
    by_request = depth.transpose(1, 0, 2)
    spread = by_request[:, :, None, :] - by_request[:, None, :, :]
    linked = reach[:, :, :, None] > 0
    factor = jnp.where(linked, jnp.exp(jnp.where(linked, spread, 0.0)), 0.0)
    weights = (factor * affinity[:, :, :, None] * step.transpose(1, 0, 2)[:, None, :, :]).astype(
        jnp.bfloat16
    )
    tree_part = jnp.einsum("rjih,irhp->jrhp", weights, inputs4, preferred_element_type=jnp.float32)
    cache_part = jnp.einsum(
        "jrn,rhpn->jrhp", reads, cache_state, preferred_element_type=jnp.float32
    )
    cache_part = cache_part * jnp.exp(depth)[:, :, :, None]
    ssm_out = (tree_part + cache_part + skip_gain[:, None] * inputs4.astype(jnp.float32)).astype(
        jnp.bfloat16
    )
    ssm_out = ssm_out.reshape(nodes, requests, columns)
    local_nodes = residual.shape[0]
    width = residual.shape[2]
    token_count = local_nodes * requests
    experts = router.shape[1]
    topk = expert_ids.shape[2]
    capacity = 2 * token_count * topk // (experts + experts // 4)
    layer_out = experts_block(
        ssm_out.reshape(nodes * requests, columns),
        out_proj,
        residual.reshape(token_count, width),
        norm_gain,
        router,
        expert_ids.reshape(token_count, topk),
        gate_proj,
        up_proj,
        down_proj,
        capacity,
    )
    return layer_out.reshape(local_nodes, requests, width)


def solution(mesh):
    in_specs = (
        P(None, ("groups", "req"), "head"),
        P("head", ("groups", "req"), None),
        P("head", ("groups", "req"), None),
        P(None, ("groups", "req"), "head"),
        P("head"),
        P("head"),
        P("head"),
        P(("groups", "req"), "head", None, None),
        P(("groups", "req"), None),
        P("head", None),
        P("head", ("groups", "req"), None),
        P(),
        P(),
        P("head", ("groups", "req"), None),
        P(("head", "req"), None, None),
        P(("head", "req"), None, None),
        P(("head", "req"), None, None),
    )
    out_specs = P("head", ("groups", "req"), None)
    return jax.shard_map(body, mesh=mesh, in_specs=in_specs, out_specs=out_specs, check_vma=False)
```

```python
import functools
import jax
import jax.numpy as jnp
from jax import lax
from jax.experimental import pallas as pl
from jax.experimental.pallas import tpu as pltpu
from jax.sharding import PartitionSpec as P

F32 = jnp.float32
BF16 = jnp.bfloat16


def ancestry(parents):
    nodes = parents.shape[1]
    labels = jnp.arange(nodes, dtype=jnp.int32)
    power = (parents[:, :, None] == labels[None, None, :]).astype(BF16)
    reach = power + jnp.eye(nodes, dtype=BF16)
    covered = 2
    while covered < nodes:
        power = jnp.einsum("rjk,rki->rji", power, power, preferred_element_type=F32).astype(BF16)
        reach = reach + jnp.einsum("rjk,rki->rji", power, reach, preferred_element_type=F32).astype(BF16)
        covered *= 2
    return reach.astype(F32)


def remote(src, dst, send, recv, head, req):
    return pltpu.make_async_remote_copy(
        src_ref=src,
        dst_ref=dst,
        send_sem=send,
        recv_sem=recv,
        device_id={"head": head, "req": req},
        device_id_type=pl.DeviceIdType.MESH,
    )


def block_kernel(
    ys, zs, cap, chunks, backs,
    ssm, proj_h, res, gain, router, ids, wg_h, wu_h, wd_h,
    out,
    part, proj, buf0, bufn, wgu, wd, smat, acc, act, cmat, ybuf, pbuf, trecv, ysend, yrecv, zsend, zrecv, mt, ms, my, am,
    p_s, mt_s, mt_r, my_s, my_r, az_s, ay_s, at_s, ar, atr, rt_s, rt_r, ry_s, ry_r, rz_s, rz_r, w_s, d_s,
):
    head = lax.axis_index("head")
    z = lax.axis_index("req")
    y = head // 2
    c = head % 2
    t = 1 - c
    twin = y * 2 + t
    rows, width = res.shape
    experts = router.shape[0]
    held, hidden = wg_h.shape[0], wg_h.shape[2]
    slots = wgu.shape[0]
    dslots = wd.shape[0]
    tokens = 2 * ys * zs * rows
    cw = width // chunks
    rw = width // backs

    def at_y(d):
        return (y + d) % ys

    flip = 1 - 2 * (2 * z // zs)

    def at_z(d):
        return (z + flip * d + zs) % zs

    def blk(yy, cc, zz):
        return (yy * 2 + cc) * zs + zz

    units = held * chunks

    def load_gu(u):
        slot = u % slots
        at = pl.ds(pl.multiple_of((u // held) * cw, cw), cw)
        return (
            pltpu.make_async_copy(wg_h.at[u % held, at, :], wgu.at[slot, :, pl.ds(0, hidden)], w_s.at[slot, 0]),
            pltpu.make_async_copy(wu_h.at[u % held, at, :], wgu.at[slot, :, pl.ds(hidden, hidden)], w_s.at[slot, 1]),
        )

    def load_d(k):
        return pltpu.make_async_copy(
            wd_h.at[:, :, pl.ds(k * rw, rw)], wd.at[k % dslots], d_s.at[k % dslots]
        )

    def load_p(k):
        return pltpu.make_async_copy(proj_h.at[:, pl.ds(k * cw, cw)], proj.at[k % 2], p_s.at[k % 2])

    load_p(0).start()
    load_p(1).start()
    barrier = pltpu.get_barrier_semaphore()
    pl.semaphore_signal(barrier, inc=1, device_id={"head": twin, "req": z}, device_id_type=pl.DeviceIdType.MESH)
    for d in range(1, ys):
        pl.semaphore_signal(barrier, inc=1, device_id={"head": at_y(d) * 2 + c, "req": z}, device_id_type=pl.DeviceIdType.MESH)
    for d in range(1, zs):
        pl.semaphore_signal(barrier, inc=1, device_id={"head": head, "req": (z + d) % zs}, device_id_type=pl.DeviceIdType.MESH)
    pl.semaphore_wait(barrier, ys + zs - 1)

    pending = []

    def mixer(k):
        load_p(k).wait()
        v = jnp.dot(ssm[...], proj[k % 2], preferred_element_type=F32)
        part[k] = v.reshape(ys, 2, rows, cw)
        if k + 2 < chunks:
            load_p(k + 2).start()
        for d in [*range(1, ys), 0]:
            cp = remote(part.at[k, at_y(d), t], mt.at[k, d], mt_s.at[k, d], mt_r.at[k, d], twin, z)
            cp.start()
            pending.append(cp)

    def mixer_y(k):
        for d in range(1, ys):
            remote(mt.at[k, d], mt.at[k, d], mt_s.at[k, d], mt_r.at[k, d], twin, z).wait_recv()
            ms[k, d] = (part[k, at_y(d), c] + mt[k, d]).astype(BF16)
            cp = remote(ms.at[k, d], my.at[k, ys - d], my_s.at[k, d], my_r.at[k, ys - d], at_y(d) * 2 + c, z)
            cp.start()
            pending.append(cp)

    for k in range(chunks):
        mixer(k)
        if k > 0:
            mixer_y(k - 1)
    for u in range(slots):
        for cp in load_gu(jnp.int32(u)):
            cp.start()
    for k in range(dslots):
        load_d(k).start()
    mixer_y(chunks - 1)
    sums = []
    for k in range(chunks):
        remote(mt.at[k, 0], mt.at[k, 0], mt_s.at[k, 0], mt_r.at[k, 0], twin, z).wait_recv()
        total = part[k, y, c] + mt[k, 0]
        for r in range(1, ys):
            remote(ms.at[k, r], my.at[k, r], my_s.at[k, r], my_r.at[k, r], at_y(r) * 2 + c, z).wait_recv()
            total = total + my[k, r].astype(F32)
        sums.append(total)
    mixed = jnp.concatenate(sums, axis=1)
    after = (res[...].astype(F32) + mixed).astype(BF16)
    am[...] = after
    wide = after.astype(F32)
    meansq = jnp.mean(wide * wide, axis=-1, keepdims=True)
    normed = (wide * lax.rsqrt(meansq + 1e-05) * gain[...]).astype(BF16)
    own = blk(y, c, z)
    nt = (((1,), (1,)), ((), ()))
    buf0[own, :, :cw] = normed[:, :cw]
    for k in range(1, chunks):
        bufn[k - 1, own] = normed[:, k * cw : (k + 1) * cw]
    logits = lax.dot_general(normed, router[...], nt, preferred_element_type=F32)
    lanes = lax.broadcasted_iota(jnp.int32, (rows, experts), 1)
    chosen = ids[...]
    named = lanes == chosen[:, 0:1]
    for k in range(1, ids.shape[1]):
        named = named | (lanes == chosen[:, k : k + 1])
    powered = jnp.where(named, jnp.exp(jnp.where(named, logits, 0.0)), 0.0)
    gate = powered / jnp.sum(powered, axis=1, keepdims=True)
    if experts < 128:
        gate = jnp.concatenate([gate, jnp.zeros((rows, 128 - experts), F32)], axis=1)
    buf0[own, :, cw:] = gate.astype(BF16)

    def block(k, b):
        return buf0.at[b] if k == 0 else bufn.at[k - 1, b]

    def pass_y(k, b, i):
        for d in range(1, ys):
            s = (d - 1) * zs + i
            cp = remote(block(k, b), block(k, b), ay_s.at[k, s], ar.at[k, b], at_y(d) * 2 + c, z)
            cp.start()
            pending.append(cp)

    def pass_twin(k, e):
        at = pl.ds(blk(at_y(e), c, 0), zs)
        ref = buf0.at[at] if k == 0 else bufn.at[k - 1, at]
        cp = remote(ref, ref, at_s.at[k, e], atr.at[k, e], twin, z)
        cp.start()
        pending.append(cp)

    def landed(k, b):
        remote(block(k, b), block(k, b), at_s.at[k, 0], ar.at[k, b], twin, z).wait_recv()

    def send_z(k):
        for d in range(1, zs):
            cp = remote(block(k, own), block(k, own), az_s.at[k, d], ar.at[k, own], head, at_z(d))
            cp.start()
            pending.append(cp)

    def relay_z(k):
        for d in range(1, zs):
            b = blk(y, c, at_z(d))
            landed(k, b)
            pass_y(k, b, d)
        pass_twin(k, 0)
        if k + 2 < chunks:
            pass_y(k + 2, own, 0)

    def relay_y(k):
        for e in range(1, ys):
            for d in range(zs):
                landed(k, blk(at_y(e), c, at_z(d)))
            pass_twin(k, e)

    def all_in(k):
        for e in range(ys):
            at = pl.ds(blk(at_y(e), t, 0), zs)
            ref = buf0.at[at] if k == 0 else bufn.at[k - 1, at]
            remote(ref, ref, at_s.at[k, e], atr.at[k, e], twin, z).wait_recv()

    def select(k):
        rows_k = (buf0[:, :, :cw] if k == 0 else bufn[k - 1]).reshape(tokens, cw)
        half = cw // 2
        for n in range(2):
            cols = slice(n * half, (n + 1) * half)
            ybuf[:, cols] = jnp.dot(smat[...], rows_k[:, cols], preferred_element_type=F32).astype(BF16)

    def apply(k, low, high):
        def expert(h, carry):
            u = k * held + h
            slot = u % slots
            x = ybuf[pl.ds(pl.multiple_of(h * cap, cap), cap), :]
            for cp in load_gu(u):
                cp.wait()
            both = jnp.dot(x, wgu[slot], preferred_element_type=F32)
            if k > 0:
                both = both + acc[h]
            if k < chunks - 1:
                acc[h] = both
            else:
                gated = both[:, :hidden]
                act[h] = (gated / (1.0 + jnp.exp(-gated)) * both[:, hidden:]).astype(BF16)

            @pl.when(u + slots < units)
            def _():
                for cp in load_gu(u + slots):
                    cp.start()

            return carry

        lax.fori_loop(low, high, expert, 0)

    for k in range(chunks):
        if k < 2:
            pass_y(k, own, 0)
        send_z(k)
    relay_z(0)
    relay_y(0)
    all_in(0)

    gates = buf0[:, :, cw:].reshape(tokens, 128)
    first = ((head * zs + z) * held) % experts
    row_of = lax.broadcasted_iota(jnp.int32, (128, 128), 0)
    lane_of = lax.broadcasted_iota(jnp.int32, (128, 128), 1)
    pick = ((lane_of == first + row_of) & (row_of < held)).astype(BF16)
    g = lax.dot_general(gates, pick, nt, preferred_element_type=F32)
    gt = lax.dot_general(pick, gates, nt, preferred_element_type=F32)
    up_t = lax.broadcasted_iota(jnp.int32, (tokens, tokens), 0)
    up_u = lax.broadcasted_iota(jnp.int32, (tokens, tokens), 1)
    before = jnp.where(up_t < up_u, 1.0, 0.0).astype(BF16)
    after_m = jnp.where(up_u < up_t, 1.0, 0.0).astype(BF16)
    on = jnp.where(g > 0, 1.0, 0.0).astype(BF16)
    ont = jnp.where(gt > 0, 1.0, 0.0).astype(BF16)
    rank = jnp.dot(after_m, on, preferred_element_type=F32)
    rankt = jnp.dot(ont, before, preferred_element_type=F32)
    rank = jnp.where(g > 0, rank, -1.0)
    rankt = jnp.where(gt > 0, rankt, -1.0)
    slot_row = lax.broadcasted_iota(jnp.int32, (cap, tokens), 0).astype(F32)
    for h in range(held):
        smat[h * cap : (h + 1) * cap, :] = jnp.where(rankt[h : h + 1, :] == slot_row, 1.0, 0.0).astype(BF16)
    select(0)
    relay_z(1)
    slot_lane = lax.broadcasted_iota(jnp.int32, (tokens, cap), 1).astype(F32)
    for h in range(held):
        col = jnp.where(rank[:, h : h + 1] == slot_lane, g[:, h : h + 1], 0.0).astype(BF16)
        col = col.reshape(ys, 2, zs * rows, cap)
        for e in range(ys):
            for cc in range(2):
                cmat[cc, e * zs * rows : (e + 1) * zs * rows, h * cap : (h + 1) * cap] = col[e, cc]

    middle = held // 2
    for k in range(chunks):
        if k > 0:
            select(k)
        apply(k, 0, middle)
        if k + 1 < chunks:
            relay_y(k + 1)
        apply(k, middle, held)
        if k + 2 < chunks:
            relay_z(k + 2)
        if k + 1 < chunks:
            all_in(k + 1)

    def produce(k):
        ks = k % dslots
        load_d(k).wait()

        def down(h, carry):
            at = pl.ds(pl.multiple_of(h * cap, cap), cap)
            ybuf[at, :rw] = jnp.dot(act[h], wd[ks, h], preferred_element_type=F32).astype(BF16)
            return carry

        lax.fori_loop(0, held, down, 0)
        if k + dslots < backs:
            load_d(k + dslots).start()

        def mix(cc):
            v = jnp.dot(cmat[cc], ybuf[:, :rw], preferred_element_type=F32).astype(BF16)
            pbuf[k, cc] = v.reshape(ys, zs, rows, rw)

        mix(t)
        for e in [*range(1, ys), 0]:
            cp = remote(pbuf.at[k, t, at_y(e)], trecv.at[k, e], rt_s.at[k, e], rt_r.at[k, e], twin, z)
            cp.start()
            pending.append(cp)
        mix(c)

    def sum_twin(k):
        for e in [*range(1, ys), 0]:
            remote(trecv.at[k, e], trecv.at[k, e], rt_s.at[k, e], rt_r.at[k, e], twin, z).wait_recv()
            mine = pbuf[k, c, at_y(e)].astype(F32)
            ysend[k, e] = (mine + trecv[k, e].astype(F32)).astype(BF16)
            if e > 0:
                cp = remote(ysend.at[k, e], yrecv.at[k, ys - e], ry_s.at[k, e], ry_r.at[k, ys - e], at_y(e) * 2 + c, z)
                cp.start()
                pending.append(cp)

    def sum_y(k):
        total = ysend[k, 0].astype(F32)
        for e in range(1, ys):
            remote(yrecv.at[k, e], yrecv.at[k, e], ry_s.at[k, e], ry_r.at[k, e], at_y(e) * 2 + c, z).wait_recv()
            total = total + yrecv[k, e].astype(F32)
        zsend[k] = total.astype(BF16)
        for d in range(1, zs):
            zz = (z + d) % zs
            cp = remote(zsend.at[k, zz], zrecv.at[k, zs - d], rz_s.at[k, d], rz_r.at[k, zs - d], head, zz)
            cp.start()
            pending.append(cp)

    def finish(k):
        total = zsend[k, z].astype(F32)
        for d in range(1, zs):
            zz = (z + d) % zs
            remote(zsend.at[k, zz], zrecv.at[k, d], rz_s.at[k, d], rz_r.at[k, d], head, zz).wait_recv()
            total = total + zrecv[k, d].astype(F32)
        cols = slice(k * rw, (k + 1) * rw)
        out[:, cols] = (am[:, cols].astype(F32) + total).astype(BF16)

    for k in range(backs):
        produce(k)
        if k == 0:
            sum_twin(k)
        elif k > 1:
            sum_twin(k - 1)
        if k >= 4:
            sum_y(k - 4)
        if k >= 6:
            finish(k - 6)
    sum_twin(backs - 1)
    for k in range(backs - 4, backs):
        sum_y(k)
        if k >= 2:
            finish(k - 2)
    finish(backs - 2)
    finish(backs - 1)
    for cp in pending:
        cp.wait_send()


def experts_block(ssm_out, out_proj, residual, norm_gain, router, ids, gate_proj, up_proj, down_proj, capacity):
    heads = lax.axis_size("head")
    zs = lax.axis_size("req")
    ys = heads // 2
    rows, width = residual.shape
    held, _, hidden = gate_proj.shape
    chunks = 4
    backs = 4
    slots = min(8, held * chunks)
    dslots = 2
    cw = width // chunks
    rw = width // backs
    blocks = heads * zs
    tokens = blocks * rows
    cap = capacity * blocks
    vmem = pl.BlockSpec(memory_space=pltpu.VMEM)
    hbm = pl.BlockSpec(memory_space=pl.ANY)
    dma = pltpu.SemaphoreType.DMA
    return pl.pallas_call(
        functools.partial(block_kernel, ys, zs, cap, chunks, backs),
        out_shape=jax.ShapeDtypeStruct((rows, width), BF16),
        in_specs=[vmem, hbm] + [vmem] * 4 + [hbm] * 3,
        out_specs=vmem,
        scratch_shapes=[
            pltpu.VMEM((chunks, ys, 2, rows, cw), F32),
            pltpu.VMEM((2, ssm_out.shape[1], cw), BF16),
            pltpu.VMEM((blocks, rows, cw + 128), BF16),
            pltpu.VMEM((chunks - 1, blocks, rows, cw), BF16),
            pltpu.VMEM((slots, cw, 2 * hidden), BF16),
            pltpu.VMEM((dslots, held, hidden, rw), BF16),
            pltpu.VMEM((held * cap, tokens), BF16),
            pltpu.VMEM((held, cap, 2 * hidden), F32),
            pltpu.VMEM((held, cap, hidden), BF16),
            pltpu.VMEM((2, ys * zs * rows, held * cap), BF16),
            pltpu.VMEM((held * cap, cw), BF16),
            pltpu.VMEM((backs, 2, ys, zs, rows, rw), BF16),
            pltpu.VMEM((backs, ys, zs, rows, rw), BF16),
            pltpu.VMEM((backs, ys, zs, rows, rw), BF16),
            pltpu.VMEM((backs, ys, zs, rows, rw), BF16),
            pltpu.VMEM((backs, zs, rows, rw), BF16),
            pltpu.VMEM((backs, zs, rows, rw), BF16),
            pltpu.VMEM((chunks, ys, rows, cw), F32),
            pltpu.VMEM((chunks, ys, rows, cw), BF16),
            pltpu.VMEM((chunks, ys, rows, cw), BF16),
            pltpu.VMEM((rows, width), BF16),
            dma((2,)), dma((chunks, ys)), dma((chunks, ys)), dma((chunks, ys)), dma((chunks, ys)),
            dma((chunks, zs)), dma((chunks, ys * zs)), dma((chunks, ys)), dma((chunks, blocks)), dma((chunks, ys)),
            dma((backs, ys)), dma((backs, ys)), dma((backs, ys)), dma((backs, ys)),
            dma((backs, zs)), dma((backs, zs)),
            dma((slots, 2)), dma((dslots,)),
        ],
        compiler_params=pltpu.CompilerParams(
            collective_id=0, has_side_effects=True, vmem_limit_bytes=62 * 2**20
        ),
    )(
        ssm_out, out_proj, residual, norm_gain.reshape(1, width), router.T, ids,
        gate_proj, up_proj, down_proj,
    )


def body(
    ssm_input,
    write_vec,
    read_vec,
    step_raw,
    step_bias,
    decay_rate,
    skip_gain,
    cache_state,
    parents,
    out_proj,
    residual,
    norm_gain,
    router,
    expert_ids,
    gate_proj,
    up_proj,
    down_proj,
):
    nodes, requests, columns = ssm_input.shape
    heads = step_raw.shape[2]
    head_size = columns // heads
    state = write_vec.shape[2]
    own = jnp.concatenate([write_vec, read_vec], axis=2)
    count = lax.axis_size("head")
    turned = [own] + [
        lax.ppermute(own, "head", [(i, (i + d) % count) for i in range(count)]) for d in range(1, count)
    ]
    ring = jnp.concatenate(turned[::-1] * 2, axis=0)
    start = (count - 1 - lax.axis_index("head")) * own.shape[0]
    both = lax.dynamic_slice_in_dim(ring, start, count * own.shape[0], axis=0)
    writes, reads = both[:, :, :state], both[:, :, state:]
    inputs4 = ssm_input.reshape(nodes, requests, heads, head_size)
    step = jax.nn.softplus(step_raw + step_bias)
    rates = -step * decay_rate
    reach = ancestry(parents)
    depth = jnp.einsum("rji,irh->jrh", reach, rates, precision=lax.Precision.HIGHEST)
    affinity = jnp.einsum("jrn,irn->rji", reads, writes, preferred_element_type=jnp.float32)
    by_request = depth.transpose(1, 0, 2)
    spread = by_request[:, :, None, :] - by_request[:, None, :, :]
    linked = reach[:, :, :, None] > 0
    factor = jnp.where(linked, jnp.exp(jnp.where(linked, spread, 0.0)), 0.0)
    weights = (factor * affinity[:, :, :, None] * step.transpose(1, 0, 2)[:, None, :, :]).astype(
        jnp.bfloat16
    )
    tree_part = jnp.einsum("rjih,irhp->jrhp", weights, inputs4, preferred_element_type=jnp.float32)
    cache_part = jnp.einsum(
        "jrn,rhpn->jrhp", reads, cache_state, preferred_element_type=jnp.float32
    )
    cache_part = cache_part * jnp.exp(depth)[:, :, :, None]
    ssm_out = (tree_part + cache_part + skip_gain[:, None] * inputs4.astype(jnp.float32)).astype(
        jnp.bfloat16
    )
    ssm_out = ssm_out.reshape(nodes, requests, columns)
    local_nodes = residual.shape[0]
    width = residual.shape[2]
    token_count = local_nodes * requests
    experts = router.shape[1]
    topk = expert_ids.shape[2]
    capacity = 2 * token_count * topk // (experts + experts // 4)
    layer_out = experts_block(
        ssm_out.reshape(nodes * requests, columns),
        out_proj,
        residual.reshape(token_count, width),
        norm_gain,
        router,
        expert_ids.reshape(token_count, topk),
        gate_proj,
        up_proj,
        down_proj,
        capacity,
    )
    return layer_out.reshape(local_nodes, requests, width)


def solution(mesh):
    in_specs = (
        P(None, ("groups", "req"), "head"),
        P("head", ("groups", "req"), None),
        P("head", ("groups", "req"), None),
        P(None, ("groups", "req"), "head"),
        P("head"),
        P("head"),
        P("head"),
        P(("groups", "req"), "head", None, None),
        P(("groups", "req"), None),
        P("head", None),
        P("head", ("groups", "req"), None),
        P(),
        P(),
        P("head", ("groups", "req"), None),
        P(("head", "req"), None, None),
        P(("head", "req"), None, None),
        P(("head", "req"), None, None),
    )
    out_specs = P("head", ("groups", "req"), None)
    return jax.shard_map(body, mesh=mesh, in_specs=in_specs, out_specs=out_specs, check_vma=False)
```

```python
import functools
import jax
import jax.numpy as jnp
from jax import lax
from jax.experimental import pallas as pl
from jax.experimental.pallas import tpu as pltpu
from jax.sharding import PartitionSpec as P

F32 = jnp.float32
BF16 = jnp.bfloat16


def ancestry(parents):
    nodes = parents.shape[1]
    labels = jnp.arange(nodes, dtype=jnp.int32)
    power = (parents[:, :, None] == labels[None, None, :]).astype(BF16)
    reach = power + jnp.eye(nodes, dtype=BF16)
    covered = 2
    while covered < nodes:
        power = jnp.einsum("rjk,rki->rji", power, power, preferred_element_type=F32).astype(BF16)
        reach = reach + jnp.einsum("rjk,rki->rji", power, reach, preferred_element_type=F32).astype(BF16)
        covered *= 2
    return reach.astype(F32)


def remote(src, dst, send, recv, head, req):
    return pltpu.make_async_remote_copy(
        src_ref=src,
        dst_ref=dst,
        send_sem=send,
        recv_sem=recv,
        device_id={"head": head, "req": req},
        device_id_type=pl.DeviceIdType.MESH,
    )


def block_kernel(
    ys, zs, cap, chunks, backs,
    ssm, proj_h, res, gain, router, ids, wg_h, wu_h, wd_h,
    out,
    part, proj, buf0, bufn, wgu, wd, smat, acc, act, cmat, ybuf, pbuf, trecv, ysend, yrecv, zsend, zrecv, mt, ms, my, am,
    p_s, mt_s, mt_r, my_s, my_r, az_s, ay_s, at_s, ar, atr, rt_s, rt_r, ry_s, ry_r, rz_s, rz_r, w_s, d_s,
):
    head = lax.axis_index("head")
    z = lax.axis_index("req")
    y = head // 2
    c = head % 2
    t = 1 - c
    twin = y * 2 + t
    rows, width = res.shape
    experts = router.shape[0]
    held, hidden = wg_h.shape[0], wg_h.shape[2]
    slots = wgu.shape[0]
    dslots = wd.shape[0]
    tokens = 2 * ys * zs * rows
    cw = width // chunks
    rw = width // backs

    def at_y(d):
        return (y + d) % ys

    flip = 1 - 2 * (2 * z // zs)

    def at_z(d):
        return (z + flip * d + zs) % zs

    def blk(yy, cc, zz):
        return (yy * 2 + cc) * zs + zz

    units = held * chunks

    def load_gu(u):
        slot = u % slots
        at = pl.ds(pl.multiple_of((u // held) * cw, cw), cw)
        return (
            pltpu.make_async_copy(wg_h.at[u % held, at, :], wgu.at[slot, :, pl.ds(0, hidden)], w_s.at[slot, 0]),
            pltpu.make_async_copy(wu_h.at[u % held, at, :], wgu.at[slot, :, pl.ds(hidden, hidden)], w_s.at[slot, 1]),
        )

    def load_d(k):
        return pltpu.make_async_copy(
            wd_h.at[:, :, pl.ds(k * rw, rw)], wd.at[k % dslots], d_s.at[k % dslots]
        )

    def load_p(k):
        return pltpu.make_async_copy(proj_h.at[:, pl.ds(k * cw, cw)], proj.at[k % 2], p_s.at[k % 2])

    load_p(0).start()
    load_p(1).start()
    barrier = pltpu.get_barrier_semaphore()
    pl.semaphore_signal(barrier, inc=1, device_id={"head": twin, "req": z}, device_id_type=pl.DeviceIdType.MESH)
    for d in range(1, ys):
        pl.semaphore_signal(barrier, inc=1, device_id={"head": at_y(d) * 2 + c, "req": z}, device_id_type=pl.DeviceIdType.MESH)
    for d in range(1, zs):
        pl.semaphore_signal(barrier, inc=1, device_id={"head": head, "req": (z + d) % zs}, device_id_type=pl.DeviceIdType.MESH)
    pl.semaphore_wait(barrier, ys + zs - 1)

    pending = []

    def mixer(k):
        load_p(k).wait()
        v = jnp.dot(ssm[...], proj[k % 2], preferred_element_type=F32)
        part[k] = v.reshape(ys, 2, rows, cw)
        if k + 2 < chunks:
            load_p(k + 2).start()
        for d in [*range(1, ys), 0]:
            cp = remote(part.at[k, at_y(d), t], mt.at[k, d], mt_s.at[k, d], mt_r.at[k, d], twin, z)
            cp.start()
            pending.append(cp)

    def mixer_y(k):
        for d in range(1, ys):
            remote(mt.at[k, d], mt.at[k, d], mt_s.at[k, d], mt_r.at[k, d], twin, z).wait_recv()
            ms[k, d] = (part[k, at_y(d), c] + mt[k, d]).astype(BF16)
            cp = remote(ms.at[k, d], my.at[k, ys - d], my_s.at[k, d], my_r.at[k, ys - d], at_y(d) * 2 + c, z)
            cp.start()
            pending.append(cp)

    for k in range(chunks):
        mixer(k)
        if k > 0:
            mixer_y(k - 1)
    for u in range(slots):
        for cp in load_gu(jnp.int32(u)):
            cp.start()
    for k in range(dslots):
        load_d(k).start()
    mixer_y(chunks - 1)
    sums = []
    for k in range(chunks):
        remote(mt.at[k, 0], mt.at[k, 0], mt_s.at[k, 0], mt_r.at[k, 0], twin, z).wait_recv()
        total = part[k, y, c] + mt[k, 0]
        for r in range(1, ys):
            remote(ms.at[k, r], my.at[k, r], my_s.at[k, r], my_r.at[k, r], at_y(r) * 2 + c, z).wait_recv()
            total = total + my[k, r].astype(F32)
        sums.append(total)
    mixed = jnp.concatenate(sums, axis=1)
    after = (res[...].astype(F32) + mixed).astype(BF16)
    am[...] = after
    wide = after.astype(F32)
    meansq = jnp.mean(wide * wide, axis=-1, keepdims=True)
    normed = (wide * lax.rsqrt(meansq + 1e-05) * gain[...]).astype(BF16)
    own = blk(y, c, z)
    nt = (((1,), (1,)), ((), ()))
    buf0[own, :, :cw] = normed[:, :cw]
    for k in range(1, chunks):
        bufn[k - 1, own] = normed[:, k * cw : (k + 1) * cw]
    logits = lax.dot_general(normed, router[...], nt, preferred_element_type=F32)
    lanes = lax.broadcasted_iota(jnp.int32, (rows, experts), 1)
    chosen = ids[...]
    named = lanes == chosen[:, 0:1]
    for k in range(1, ids.shape[1]):
        named = named | (lanes == chosen[:, k : k + 1])
    powered = jnp.where(named, jnp.exp(jnp.where(named, logits, 0.0)), 0.0)
    gate = powered / jnp.sum(powered, axis=1, keepdims=True)
    if experts < 128:
        gate = jnp.concatenate([gate, jnp.zeros((rows, 128 - experts), F32)], axis=1)
    buf0[own, :, cw:] = gate.astype(BF16)

    def block(k, b):
        return buf0.at[b] if k == 0 else bufn.at[k - 1, b]

    def pass_y(k, b, i):
        for d in range(1, ys):
            s = (d - 1) * zs + i
            cp = remote(block(k, b), block(k, b), ay_s.at[k, s], ar.at[k, b], at_y(d) * 2 + c, z)
            cp.start()
            pending.append(cp)

    def pass_twin(k, e):
        at = pl.ds(blk(at_y(e), c, 0), zs)
        ref = buf0.at[at] if k == 0 else bufn.at[k - 1, at]
        cp = remote(ref, ref, at_s.at[k, e], atr.at[k, e], twin, z)
        cp.start()
        pending.append(cp)

    def landed(k, b):
        remote(block(k, b), block(k, b), at_s.at[k, 0], ar.at[k, b], twin, z).wait_recv()

    def send_z(k):
        for d in range(1, zs):
            cp = remote(block(k, own), block(k, own), az_s.at[k, d], ar.at[k, own], head, at_z(d))
            cp.start()
            pending.append(cp)

    def relay_z(k):
        for d in range(1, zs):
            b = blk(y, c, at_z(d))
            landed(k, b)
            pass_y(k, b, d)
        pass_twin(k, 0)
        if k + 2 < chunks:
            pass_y(k + 2, own, 0)

    def relay_y(k):
        for e in range(1, ys):
            for d in range(zs):
                landed(k, blk(at_y(e), c, at_z(d)))
            pass_twin(k, e)

    def all_in(k):
        for e in range(ys):
            at = pl.ds(blk(at_y(e), t, 0), zs)
            ref = buf0.at[at] if k == 0 else bufn.at[k - 1, at]
            remote(ref, ref, at_s.at[k, e], atr.at[k, e], twin, z).wait_recv()

    def select(k):
        rows_k = (buf0[:, :, :cw] if k == 0 else bufn[k - 1]).reshape(tokens, cw)
        half = cw // 2
        for n in range(2):
            cols = slice(n * half, (n + 1) * half)
            ybuf[:, cols] = jnp.dot(smat[...], rows_k[:, cols], preferred_element_type=F32).astype(BF16)

    def apply(k, low, high):
        def expert(h, carry):
            u = k * held + h
            slot = u % slots
            x = ybuf[pl.ds(pl.multiple_of(h * cap, cap), cap), :]
            for cp in load_gu(u):
                cp.wait()
            both = jnp.dot(x, wgu[slot], preferred_element_type=F32)
            if k > 0:
                both = both + acc[h]
            if k < chunks - 1:
                acc[h] = both
            else:
                gated = both[:, :hidden]
                act[h] = (gated / (1.0 + jnp.exp(-gated)) * both[:, hidden:]).astype(BF16)

            @pl.when(u + slots < units)
            def _():
                for cp in load_gu(u + slots):
                    cp.start()

            return carry

        lax.fori_loop(low, high, expert, 0)

    for k in range(chunks):
        if k < 2:
            pass_y(k, own, 0)
        send_z(k)
    relay_z(0)
    relay_y(0)
    all_in(0)
    relay_z(1)

    gates = buf0[:, :, cw:].reshape(tokens, 128)
    first = ((head * zs + z) * held) % experts
    row_of = lax.broadcasted_iota(jnp.int32, (128, 128), 0)
    lane_of = lax.broadcasted_iota(jnp.int32, (128, 128), 1)
    pick = ((lane_of == first + row_of) & (row_of < held)).astype(BF16)
    g = lax.dot_general(gates, pick, nt, preferred_element_type=F32)
    gt = lax.dot_general(pick, gates, nt, preferred_element_type=F32)
    up_t = lax.broadcasted_iota(jnp.int32, (tokens, tokens), 0)
    up_u = lax.broadcasted_iota(jnp.int32, (tokens, tokens), 1)
    before = jnp.where(up_t < up_u, 1.0, 0.0).astype(BF16)
    after_m = jnp.where(up_u < up_t, 1.0, 0.0).astype(BF16)
    on = jnp.where(g > 0, 1.0, 0.0).astype(BF16)
    ont = jnp.where(gt > 0, 1.0, 0.0).astype(BF16)
    rank = jnp.dot(after_m, on, preferred_element_type=F32)
    rankt = jnp.dot(ont, before, preferred_element_type=F32)
    rank = jnp.where(g > 0, rank, -1.0)
    rankt = jnp.where(gt > 0, rankt, -1.0)
    slot_row = lax.broadcasted_iota(jnp.int32, (cap, tokens), 0).astype(F32)
    for h in range(held):
        smat[h * cap : (h + 1) * cap, :] = jnp.where(rankt[h : h + 1, :] == slot_row, 1.0, 0.0).astype(BF16)
    select(0)
    slot_lane = lax.broadcasted_iota(jnp.int32, (tokens, cap), 1).astype(F32)
    for h in range(held):
        col = jnp.where(rank[:, h : h + 1] == slot_lane, g[:, h : h + 1], 0.0).astype(BF16)
        col = col.reshape(ys, 2, zs * rows, cap)
        for e in range(ys):
            for cc in range(2):
                cmat[cc, e * zs * rows : (e + 1) * zs * rows, h * cap : (h + 1) * cap] = col[e, cc]

    middle = held // 2
    for k in range(chunks):
        if k > 0:
            select(k)
        apply(k, 0, middle)
        if k + 1 < chunks:
            relay_y(k + 1)
        apply(k, middle, held)
        if k + 2 < chunks:
            relay_z(k + 2)
        if k + 1 < chunks:
            all_in(k + 1)

    def produce(k):
        ks = k % dslots
        load_d(k).wait()

        def down(h, carry):
            at = pl.ds(pl.multiple_of(h * cap, cap), cap)
            ybuf[at, :rw] = jnp.dot(act[h], wd[ks, h], preferred_element_type=F32).astype(BF16)
            return carry

        lax.fori_loop(0, held, down, 0)
        if k + dslots < backs:
            load_d(k + dslots).start()

        def mix(cc):
            v = jnp.dot(cmat[cc], ybuf[:, :rw], preferred_element_type=F32).astype(BF16)
            pbuf[k, cc] = v.reshape(ys, zs, rows, rw)

        mix(t)
        for e in [*range(1, ys), 0]:
            cp = remote(pbuf.at[k, t, at_y(e)], trecv.at[k, e], rt_s.at[k, e], rt_r.at[k, e], twin, z)
            cp.start()
            pending.append(cp)
        mix(c)

    def sum_twin(k):
        for e in [*range(1, ys), 0]:
            remote(trecv.at[k, e], trecv.at[k, e], rt_s.at[k, e], rt_r.at[k, e], twin, z).wait_recv()
            mine = pbuf[k, c, at_y(e)].astype(F32)
            ysend[k, e] = (mine + trecv[k, e].astype(F32)).astype(BF16)
            if e > 0:
                cp = remote(ysend.at[k, e], yrecv.at[k, ys - e], ry_s.at[k, e], ry_r.at[k, ys - e], at_y(e) * 2 + c, z)
                cp.start()
                pending.append(cp)

    def sum_y(k):
        total = ysend[k, 0].astype(F32)
        for e in range(1, ys):
            remote(yrecv.at[k, e], yrecv.at[k, e], ry_s.at[k, e], ry_r.at[k, e], at_y(e) * 2 + c, z).wait_recv()
            total = total + yrecv[k, e].astype(F32)
        zsend[k] = total.astype(BF16)
        for d in range(1, zs):
            zz = (z + d) % zs
            cp = remote(zsend.at[k, zz], zrecv.at[k, zs - d], rz_s.at[k, d], rz_r.at[k, zs - d], head, zz)
            cp.start()
            pending.append(cp)

    def finish(k):
        total = zsend[k, z].astype(F32)
        for d in range(1, zs):
            zz = (z + d) % zs
            remote(zsend.at[k, zz], zrecv.at[k, d], rz_s.at[k, d], rz_r.at[k, d], head, zz).wait_recv()
            total = total + zrecv[k, d].astype(F32)
        cols = slice(k * rw, (k + 1) * rw)
        out[:, cols] = (am[:, cols].astype(F32) + total).astype(BF16)

    for k in range(backs):
        produce(k)
        if k == 0:
            sum_twin(k)
        elif k > 1:
            sum_twin(k - 1)
        if k >= 4:
            sum_y(k - 4)
        if k >= 6:
            finish(k - 6)
    sum_twin(backs - 1)
    for k in range(backs - 4, backs):
        sum_y(k)
        if k >= 2:
            finish(k - 2)
    finish(backs - 2)
    finish(backs - 1)
    for cp in pending:
        cp.wait_send()


def experts_block(ssm_out, out_proj, residual, norm_gain, router, ids, gate_proj, up_proj, down_proj, capacity):
    heads = lax.axis_size("head")
    zs = lax.axis_size("req")
    ys = heads // 2
    rows, width = residual.shape
    held, _, hidden = gate_proj.shape
    chunks = 4
    backs = 4
    slots = min(8, held * chunks)
    dslots = 2
    cw = width // chunks
    rw = width // backs
    blocks = heads * zs
    tokens = blocks * rows
    cap = capacity * blocks
    vmem = pl.BlockSpec(memory_space=pltpu.VMEM)
    hbm = pl.BlockSpec(memory_space=pl.ANY)
    dma = pltpu.SemaphoreType.DMA
    return pl.pallas_call(
        functools.partial(block_kernel, ys, zs, cap, chunks, backs),
        out_shape=jax.ShapeDtypeStruct((rows, width), BF16),
        in_specs=[vmem, hbm] + [vmem] * 4 + [hbm] * 3,
        out_specs=vmem,
        scratch_shapes=[
            pltpu.VMEM((chunks, ys, 2, rows, cw), F32),
            pltpu.VMEM((2, ssm_out.shape[1], cw), BF16),
            pltpu.VMEM((blocks, rows, cw + 128), BF16),
            pltpu.VMEM((chunks - 1, blocks, rows, cw), BF16),
            pltpu.VMEM((slots, cw, 2 * hidden), BF16),
            pltpu.VMEM((dslots, held, hidden, rw), BF16),
            pltpu.VMEM((held * cap, tokens), BF16),
            pltpu.VMEM((held, cap, 2 * hidden), F32),
            pltpu.VMEM((held, cap, hidden), BF16),
            pltpu.VMEM((2, ys * zs * rows, held * cap), BF16),
            pltpu.VMEM((held * cap, cw), BF16),
            pltpu.VMEM((backs, 2, ys, zs, rows, rw), BF16),
            pltpu.VMEM((backs, ys, zs, rows, rw), BF16),
            pltpu.VMEM((backs, ys, zs, rows, rw), BF16),
            pltpu.VMEM((backs, ys, zs, rows, rw), BF16),
            pltpu.VMEM((backs, zs, rows, rw), BF16),
            pltpu.VMEM((backs, zs, rows, rw), BF16),
            pltpu.VMEM((chunks, ys, rows, cw), F32),
            pltpu.VMEM((chunks, ys, rows, cw), BF16),
            pltpu.VMEM((chunks, ys, rows, cw), BF16),
            pltpu.VMEM((rows, width), BF16),
            dma((2,)), dma((chunks, ys)), dma((chunks, ys)), dma((chunks, ys)), dma((chunks, ys)),
            dma((chunks, zs)), dma((chunks, ys * zs)), dma((chunks, ys)), dma((chunks, blocks)), dma((chunks, ys)),
            dma((backs, ys)), dma((backs, ys)), dma((backs, ys)), dma((backs, ys)),
            dma((backs, zs)), dma((backs, zs)),
            dma((slots, 2)), dma((dslots,)),
        ],
        compiler_params=pltpu.CompilerParams(
            collective_id=0, has_side_effects=True, vmem_limit_bytes=62 * 2**20
        ),
    )(
        ssm_out, out_proj, residual, norm_gain.reshape(1, width), router.T, ids,
        gate_proj, up_proj, down_proj,
    )


def body(
    ssm_input,
    write_vec,
    read_vec,
    step_raw,
    step_bias,
    decay_rate,
    skip_gain,
    cache_state,
    parents,
    out_proj,
    residual,
    norm_gain,
    router,
    expert_ids,
    gate_proj,
    up_proj,
    down_proj,
):
    nodes, requests, columns = ssm_input.shape
    heads = step_raw.shape[2]
    head_size = columns // heads
    state = write_vec.shape[2]
    own = jnp.concatenate([write_vec, read_vec], axis=2)
    count = lax.axis_size("head")
    turned = [own] + [
        lax.ppermute(own, "head", [(i, (i + d) % count) for i in range(count)]) for d in range(1, count)
    ]
    ring = jnp.concatenate(turned[::-1] * 2, axis=0)
    start = (count - 1 - lax.axis_index("head")) * own.shape[0]
    both = lax.dynamic_slice_in_dim(ring, start, count * own.shape[0], axis=0)
    writes, reads = both[:, :, :state], both[:, :, state:]
    inputs4 = ssm_input.reshape(nodes, requests, heads, head_size)
    step = jax.nn.softplus(step_raw + step_bias)
    rates = -step * decay_rate
    reach = ancestry(parents)
    depth = jnp.einsum("rji,irh->jrh", reach, rates, precision=lax.Precision.HIGHEST)
    affinity = jnp.einsum("jrn,irn->rji", reads, writes, preferred_element_type=jnp.float32)
    by_request = depth.transpose(1, 0, 2)
    spread = by_request[:, :, None, :] - by_request[:, None, :, :]
    linked = reach[:, :, :, None] > 0
    factor = jnp.where(linked, jnp.exp(jnp.where(linked, spread, 0.0)), 0.0)
    weights = (factor * affinity[:, :, :, None] * step.transpose(1, 0, 2)[:, None, :, :]).astype(
        jnp.bfloat16
    )
    tree_part = jnp.einsum("rjih,irhp->jrhp", weights, inputs4, preferred_element_type=jnp.float32)
    cache_part = jnp.einsum(
        "jrn,rhpn->jrhp", reads, cache_state, preferred_element_type=jnp.float32
    )
    cache_part = cache_part * jnp.exp(depth)[:, :, :, None]
    ssm_out = (tree_part + cache_part + skip_gain[:, None] * inputs4.astype(jnp.float32)).astype(
        jnp.bfloat16
    )
    ssm_out = ssm_out.reshape(nodes, requests, columns)
    local_nodes = residual.shape[0]
    width = residual.shape[2]
    token_count = local_nodes * requests
    experts = router.shape[1]
    topk = expert_ids.shape[2]
    capacity = 2 * token_count * topk // (experts + experts // 4)
    layer_out = experts_block(
        ssm_out.reshape(nodes * requests, columns),
        out_proj,
        residual.reshape(token_count, width),
        norm_gain,
        router,
        expert_ids.reshape(token_count, topk),
        gate_proj,
        up_proj,
        down_proj,
        capacity,
    )
    return layer_out.reshape(local_nodes, requests, width)


def solution(mesh):
    in_specs = (
        P(None, ("groups", "req"), "head"),
        P("head", ("groups", "req"), None),
        P("head", ("groups", "req"), None),
        P(None, ("groups", "req"), "head"),
        P("head"),
        P("head"),
        P("head"),
        P(("groups", "req"), "head", None, None),
        P(("groups", "req"), None),
        P("head", None),
        P("head", ("groups", "req"), None),
        P(),
        P(),
        P("head", ("groups", "req"), None),
        P(("head", "req"), None, None),
        P(("head", "req"), None, None),
        P(("head", "req"), None, None),
    )
    out_specs = P("head", ("groups", "req"), None)
    return jax.shard_map(body, mesh=mesh, in_specs=in_specs, out_specs=out_specs, check_vma=False)
```
